32 devices in a mesh: ctx: 8 (over y, x, core), ch: 4 (over z).
Axes of the slice: x: 2, y: 2, z: 4, core: 2. Of those that a mesh axis runs over, the one named last changes fastest.
Arguments:
- projected: bfloat16 [3, 1536, 4096], P(None, 'ctx', 'ch'), may hold values from -6 to 6
- short_filter: float32 [7, 3, 4096], P(None, None, 'ch'), may hold values from -2.5 to 2.5
- medium_filter: bfloat16 [128, 4096], P(None, 'ch'), may hold values from -1.25 to 1.25
- decay: float32 [16, 4096], P(None, 'ch'), may hold values from 0.00013020834 to 0.05
- residues: float32 [16, 4096], P(None, 'ch'), may hold values from -3 to 3
- skip_gain: float32 [4096], P('ch'), may hold values from -6 to 6
- out_gain: float32 [4096], P('ch'), may hold values from 0.25 to 1.75
Outputs:
- mixed: bfloat16 [1536, 4096], P('ctx', 'ch')
The draws below stay inside these ranges and needn't reach their ends.
All inputs are finite; a program needn't handle non-finite values.
Results may differ from the reference program's by a relative error of at most 0.014.
Values may be sent and summed in bfloat16 or wider, within the bound.
A program may use at most 128 MiB of HBM per device.

```python
import math
import jax
import jax.numpy as jnp
from jax import lax

C = 4096
SHORT = 7
MED = 128
MODES = 16
TOKENS = 1536


def draw_medium_filter(key, part):
    key = jax.random.fold_in(key, 7)
    first_key, second_key = jax.random.split(key)
    column = jnp.arange(C).astype(jnp.float32) / C
    spread = jax.random.uniform(second_key, (1, C), jnp.float32)
    base = jnp.clip(jax.random.normal(first_key, (MED, C), jnp.float32), -4.0, 4.0)
    channel_scale = jnp.exp(jnp.log(10.0) * 0.5 * (column[None, :] + spread))
    return (base * channel_scale / (3.0 * jnp.sqrt(float(MED)))).astype(jnp.bfloat16)


def block_scale(stream_key, shape, cuts, least, high):
    gain = 1.0
    for dim, shards_of in cuts:
        draws = jax.random.uniform(jax.random.fold_in(jax.random.fold_in(stream_key, 6), dim), (shards_of,), jnp.float32, least / len(cuts), high / len(cuts))
        gain = gain * jnp.repeat(jnp.exp(draws), shape[dim] // shards_of).reshape((-1,) + (1,) * (len(shape) - 1 - dim))
    return gain


def bell_draw(stream_key, dims, scale, reach, cuts=(), kind=jnp.bfloat16):
    array = jax.random.normal(stream_key, dims, jnp.float32) * scale
    if len(cuts) > 0:
        array = block_scale(stream_key, dims, cuts, -0.22, 0.18) * array
    return jnp.clip(array, min=-reach, max=reach).astype(kind)


def setup_inputs(seed: int = 0) -> dict:
    keys = jax.random.split(jax.random.key(seed), 8)
    projected = bell_draw(keys[0], (3, TOKENS, C), 1.0, 6.0, ((1, 8), (2, 4)))
    short_filter = bell_draw(keys[1], (SHORT, 3, C), 0.4, 2.5, ((2, 4),), jnp.float32)
    medium_filter = draw_medium_filter(jax.random.fold_in(keys[7], 71), 0)
    decay = jnp.clip(jnp.exp(math.log(0.05) - 5.9506425 * jax.random.uniform(keys[3], (MODES, C), jnp.float32) ** block_scale(keys[3], (MODES, C), ((1, 4),), -0.2, 0.2)), 0.00013020834, 0.05)
    residues = bell_draw(keys[4], (MODES, C), 0.5, 3.0, ((1, 4),), jnp.float32)
    skip_gain = bell_draw(keys[5], (C,), 1.0, 6.0, ((0, 4),), jnp.float32)
    out_gain = jnp.clip(1.0 + 0.15 * jax.random.normal(keys[6], (C,), jnp.float32), 0.25, 1.75)
    return {"projected": projected, "short_filter": short_filter, "medium_filter": medium_filter, "decay": decay, "residues": residues, "skip_gain": skip_gain, "out_gain": out_gain}


norm_eps = 1e-06

def causal_taps(series, tap_weights):
    length = series.shape[0]
    padded = jnp.pad(series, ((SHORT - 1, 0), (0, 0)))
    running = jnp.zeros(series.shape, jnp.float32)
    for delay_step in range(SHORT):
        offset_row = SHORT - 1 - delay_step
        running = running + tap_weights[delay_step][None, :] * padded[offset_row:offset_row + length]
    return running

def causal_fft(signal, kernel):
    length = signal.shape[0]
    spectra = jnp.fft.rfft(signal, n=2 * length, axis=0) * jnp.fft.rfft(kernel, n=2 * length, axis=0)
    return jnp.fft.irfft(spectra, n=2 * length, axis=0)[:length]

def reference(projected, short_filter, medium_filter, decay, residues, skip_gain, out_gain):
    group_width = math.gcd(C, 512)
    group_count = C // group_width
    delays = jnp.arange(TOKENS).astype(jnp.float32)[:, None]

    def one_group(group_index):
        first_col = (group_index * group_width).astype(jnp.int32)
        inputs_part = lax.dynamic_slice_in_dim(projected, first_col, group_width, 2).astype(jnp.float32)
        short_part = lax.dynamic_slice_in_dim(short_filter, first_col, group_width, 2)
        featured = jnp.stack([causal_taps(inputs_part[stream_index], short_part[:, stream_index]) for stream_index in range(3)])
        featured = lax.optimization_barrier(featured.astype(jnp.bfloat16)).astype(jnp.float32)
        queries = featured[0]
        product = (featured[1] * featured[2]).astype(jnp.bfloat16)
        medium_part = lax.dynamic_slice_in_dim(medium_filter, first_col, group_width, 1).astype(jnp.float32)
        mediated = causal_fft(product.astype(jnp.float32), medium_part).astype(jnp.bfloat16)
        mediated = lax.optimization_barrier(mediated).astype(jnp.float32)
        decay_rates = lax.dynamic_slice_in_dim(decay, first_col, group_width, 1)
        weights = lax.dynamic_slice_in_dim(residues, first_col, group_width, 1) * jnp.sqrt(-jnp.expm1(-2.0 * decay_rates))
        kernel = jnp.zeros((TOKENS, group_width), jnp.float32)
        for mode_index in range(MODES):
            kernel = kernel + weights[mode_index][None, :] * jnp.exp(-decay_rates[mode_index][None, :] * delays)
        skip_part = lax.dynamic_slice_in_dim(skip_gain, first_col, group_width, 0)
        summed = causal_fft(mediated, kernel) + skip_part[None, :] * mediated
        return queries * summed
    mixed_groups = lax.map(one_group, jnp.arange(group_count).astype(jnp.int32))
    gated_all = jnp.transpose(mixed_groups, (1, 0, 2)).reshape(TOKENS, C)
    mean_square = lax.optimization_barrier(jnp.sum(gated_all * gated_all, axis=1, keepdims=True)) / C
    return (gated_all * lax.rsqrt(mean_square + norm_eps) * out_gain[None, :]).astype(jnp.bfloat16)
```

```python
import functools

import jax
import jax.numpy as jnp
from jax import lax
from jax.experimental import pallas as pl
from jax.experimental.pallas import tpu as pltpu
from jax.sharding import PartitionSpec as P

C = 4096
SHORT = 7
MED = 128
MODES = 16
LANES = 128
SUB = 8
LEAD = 8
TILE = 16
TAPS = 8
norm_eps = 1e-06
MESH = pl.DeviceIdType.MESH


def as_tokens(rows):
    return rows.reshape(rows.shape[0] // SUB, SUB, LANES)


def as_rows(tokens):
    return tokens.reshape(tokens.shape[0] * SUB, LANES)


def token_rows(first, count):
    start = first * SUB
    if not isinstance(start, int):
        start = pl.multiple_of(start, SUB)
    return pl.ds(start, count * SUB)


def rounded(tokens):
    return as_tokens(as_rows(tokens).astype(jnp.bfloat16).astype(jnp.float32))


def mode_sum(parts):
    count = parts.shape[0]
    while count > 1:
        count //= 2
        parts = parts[:count] + parts[count:]
    return parts[0]


def block_kernel(
    ctx_size,
    ch_size,
    proj_ref,
    short_ref,
    medium_ref,
    decay_ref,
    residue_ref,
    skip_ref,
    gain_ref,
    out_ref,
    series0,
    series1,
    series2,
    short_taps,
    medium_taps,
    product,
    queries,
    mediated,
    summed,
    rates,
    weights_buf,
    carry,
    squares,
    edge_recv,
    product_send,
    product_recv,
    state_send,
    state_recv,
    sum_send,
    sum_recv,
    edge_sems,
    product_sems,
    state_send_sems,
    state_recv_sems,
    sum_send_sems,
    sum_recv_sems,
):
    rows = proj_ref.shape[1]
    groups = proj_ref.shape[2] // LANES
    series = (series0, series1, series2)
    me = lax.axis_index("ctx")
    my_ch = lax.axis_index("ch")
    following = lax.rem(me + 1, ctx_size)

    barrier = pltpu.get_barrier_semaphore()
    for step in range(1, ctx_size):
        pl.semaphore_signal(
            barrier,
            inc=1,
            device_id={"ctx": lax.rem(me + step, ctx_size)},
            device_id_type=MESH,
        )
    for step in range(1, ch_size):
        pl.semaphore_signal(
            barrier,
            inc=1,
            device_id={"ch": lax.rem(my_ch + step, ch_size)},
            device_id_type=MESH,
        )

    if groups < SUB:
        for ref in (
            series0, series1, series2, short_taps, medium_taps, rates, weights_buf,
        ):
            ref[...] = jnp.zeros(ref.shape, ref.dtype)

    def lane_group(group):
        return slice(group * LANES, (group + 1) * LANES)

    def spread_series(index):
        @pl.loop(0, rows // TILE)
        def _(tile):
            first = pl.multiple_of(tile * TILE, TILE)
            for group in range(groups):
                part = proj_ref[index, pl.ds(first, TILE), lane_group(group)]
                series[index][
                    pl.ds((LEAD + first) * SUB + group, TILE, stride=SUB), :
                ] = part.astype(jnp.float32)

    for delay in range(SHORT):
        for group in range(groups):
            short_taps[pl.ds(delay * 3 * SUB + group, 3, stride=SUB), :] = short_ref[
                delay, :, lane_group(group)
            ]
    spread_series(1)
    spread_series(2)

    pl.semaphore_wait(barrier, ctx_size - 1 + ch_size - 1)

    edge_copy = pltpu.make_async_remote_copy(
        src_ref=proj_ref.at[:, pl.ds(rows - TILE, TILE), :],
        dst_ref=edge_recv,
        send_sem=edge_sems.at[0],
        recv_sem=edge_sems.at[1],
        device_id={"ctx": following},
        device_id_type=MESH,
    )
    product_copy = pltpu.make_async_remote_copy(
        src_ref=product_send,
        dst_ref=product_recv,
        send_sem=product_sems.at[0],
        recv_sem=product_sems.at[1],
        device_id={"ctx": following},
        device_id_type=MESH,
    )

    @pl.when(me < ctx_size - 1)
    def _():
        edge_copy.start()

    def featured(index, first):
        window = as_tokens(series[index][token_rows(LEAD + first - (SHORT - 1), TILE + SHORT - 1), :])
        total = None
        for delay in range(SHORT):
            tap = short_taps[(delay * 3 + index) * SUB : (delay * 3 + index + 1) * SUB, :]
            offset = SHORT - 1 - delay
            term = tap[None] * window[offset : offset + TILE]
            total = term if total is None else total + term
        return rounded(total)

    def product_tile(first):
        return as_rows(featured(1, first) * featured(2, first)).astype(jnp.bfloat16)

    own_first = rows - MED

    @pl.loop(own_first // TILE, rows // TILE)
    def _(tile):
        first = tile * TILE
        value = product_tile(first)
        product_send[
            pl.ds(pl.multiple_of((first - own_first) * SUB, TILE * SUB), TILE * SUB), :
        ] = value
        product[token_rows(MED + first, TILE), :] = value.astype(jnp.float32)

    @pl.when(me < ctx_size - 1)
    def _():
        product_copy.start()

    @pl.loop(0, MED // TILE)
    def _(tile):
        first = pl.multiple_of(tile * TILE, TILE)
        for group in range(groups):
            part = medium_ref[pl.ds(first, TILE), lane_group(group)]
            medium_taps[pl.ds(first * SUB + group, TILE, stride=SUB), :] = part.astype(jnp.float32)

    spread_series(0)

    for group in range(groups):
        rate = decay_ref[:, lane_group(group)]
        twice = 2.0 * rate
        series_form = twice * (
            1.0
            - twice
            * (0.5 - twice * (1.0 / 6.0 - twice * (1.0 / 24.0 - twice * (1.0 / 120.0 - twice / 720.0))))
        )
        power = jnp.where(twice < 0.125, series_form, 1.0 - jnp.exp(-twice))
        rates[pl.ds(group, MODES, stride=SUB), :] = rate
        weights_buf[pl.ds(group, MODES, stride=SUB), :] = residue_ref[
            :, lane_group(group)
        ] * jnp.sqrt(power)

    @pl.when(me > 0)
    def _():
        edge_copy.wait_recv()
        for index in range(3):
            for group in range(groups):
                part = edge_recv[index, :, lane_group(group)].astype(jnp.float32)
                series[index][pl.ds(group, LEAD, stride=SUB), :] = part[TILE - LEAD :]

    @pl.when(me == 0)
    def _():
        for index in range(3):
            series[index][0 : LEAD * SUB, :] = jnp.zeros((LEAD * SUB, LANES), jnp.float32)

    @pl.loop(0, own_first // TILE)
    def _(tile):
        first = tile * TILE
        product[token_rows(MED + first, TILE), :] = product_tile(first).astype(jnp.float32)

    @pl.loop(0, rows // TILE)
    def _(tile):
        first = tile * TILE
        queries[token_rows(first, TILE), :] = as_rows(featured(0, first))

    def medium_tile(tile):
        first = tile * TILE

        def add_taps(step, total):
            delay = step * TAPS
            window = as_tokens(
                product[token_rows(MED + first - delay - (TAPS - 1), TILE + TAPS - 1), :]
            )
            taps = as_tokens(medium_taps[token_rows(delay, TAPS), :])
            for within in range(TAPS):
                offset = TAPS - 1 - within
                total = total + taps[within][None] * window[offset : offset + TILE]
            return total

        total = lax.fori_loop(
            0, MED // TAPS, add_taps, jnp.zeros((TILE, SUB, LANES), jnp.float32)
        )
        mediated[token_rows(first, TILE), :] = as_rows(rounded(total))

    @pl.loop(MED // TILE, rows // TILE)
    def _(tile):
        medium_tile(tile)

    @pl.when(me > 0)
    def _():
        product_copy.wait_recv()

        @pl.loop(0, MED // TILE)
        def _(tile):
            start = pl.multiple_of(tile * TILE * SUB, TILE * SUB)
            part = product_recv[pl.ds(start, TILE * SUB), :]
            product[pl.ds(start, TILE * SUB), :] = part.astype(jnp.float32)

    @pl.when(me == 0)
    def _():
        product[0 : MED * SUB, :] = jnp.zeros((MED * SUB, LANES), jnp.float32)

    @pl.loop(0, MED // TILE)
    def _(tile):
        medium_tile(tile)

    decay_step = jnp.exp(-as_tokens(rates[...]))
    weights = as_tokens(weights_buf[...])

    def state_step(step, state):
        inputs = as_tokens(mediated[token_rows(step * SUB, SUB), :])
        for within in range(SUB):
            state = decay_step * state + inputs[within][None]
        return state

    zero_state = jnp.zeros((MODES, SUB, LANES), jnp.float32)
    final = lax.fori_loop(0, rows // SUB, state_step, zero_state)
    state_send[...] = as_rows(final).astype(jnp.bfloat16)

    def state_copy(step):
        return pltpu.make_async_remote_copy(
            src_ref=state_send,
            dst_ref=state_recv.at[step - 1],
            send_sem=state_send_sems.at[step - 1],
            recv_sem=state_recv_sems.at[step - 1],
            device_id={"ctx": lax.rem(me + step, ctx_size)},
            device_id_type=MESH,
        )

    for step in range(1, ctx_size):
        @pl.when(me + step < ctx_size)
        def _():
            state_copy(step).start()

    skip = skip_ref[...]
    if groups < SUB:
        skip = jnp.concatenate([skip, jnp.zeros((SUB - groups, LANES), jnp.float32)], 0)

    def local_step(step, state):
        inputs = as_tokens(mediated[token_rows(step * SUB, SUB), :])
        sums = []
        for within in range(SUB):
            state = decay_step * state + inputs[within][None]
            sums.append((mode_sum(weights * state) + skip * inputs[within])[None])
        summed[token_rows(step * SUB, SUB), :] = as_rows(jnp.concatenate(sums, 0))
        return state

    lax.fori_loop(0, rows // SUB, local_step, zero_state)

    carry[...] = jnp.zeros(carry.shape, jnp.float32)
    for step in reversed(range(1, ctx_size)):
        @pl.when(me >= step)
        def _():
            state_copy(step).wait_recv()
            span = jnp.exp(-float(rows) * rates[...])
            carry[...] = carry[...] * span + state_recv[step - 1].astype(jnp.float32)

    def carried_step(step, state):
        queried = as_tokens(queries[token_rows(step * SUB, SUB), :])
        local = as_tokens(summed[token_rows(step * SUB, SUB), :])
        gated = []
        for within in range(SUB):
            state = decay_step * state
            gated.append((queried[within] * (local[within] + mode_sum(state)))[None])
        summed[token_rows(step * SUB, SUB), :] = as_rows(jnp.concatenate(gated, 0))
        return state

    lax.fori_loop(0, rows // SUB, carried_step, weights * as_tokens(carry[...]))

    padded = squares.shape[0]
    if padded > rows:
        squares[rows:padded, :] = jnp.zeros((padded - rows, LANES), jnp.float32)

    @pl.loop(0, rows // SUB)
    def _(tile):
        first = pl.multiple_of(tile * SUB, SUB)
        total = None
        for group in range(groups):
            part = summed[pl.ds(first * SUB + group, SUB, stride=SUB), :]
            total = part * part if total is None else total + part * part
        squares[pl.ds(first, SUB), :] = total

    own_sum = lax.dot_general(
        jnp.ones((SUB, LANES), jnp.float32),
        squares[...],
        (((1,), (1,)), ((), ())),
        precision=lax.Precision.HIGHEST,
        preferred_element_type=jnp.float32,
    )
    sum_send[...] = own_sum

    def sum_copy(step):
        return pltpu.make_async_remote_copy(
            src_ref=sum_send,
            dst_ref=sum_recv.at[step - 1],
            send_sem=sum_send_sems.at[step - 1],
            recv_sem=sum_recv_sems.at[step - 1],
            device_id={"ch": lax.rem(my_ch + step, ch_size)},
            device_id_type=MESH,
        )

    for step in range(1, ch_size):
        sum_copy(step).start()
    total_sum = own_sum
    for step in range(1, ch_size):
        sum_copy(step).wait_recv()
        total_sum = total_sum + sum_recv[step - 1]
    inverse = lax.rsqrt(total_sum / C + norm_eps)
    same = lax.broadcasted_iota(jnp.int32, (padded, padded), 0) == lax.broadcasted_iota(
        jnp.int32, (padded, padded), 1
    )
    column = jnp.sum(
        jnp.where(same, jnp.broadcast_to(inverse[0:1], (padded, padded)), 0.0), 1, keepdims=True
    )
    squares[...] = jnp.broadcast_to(column, (padded, LANES))

    @pl.loop(0, rows // TILE)
    def _(tile):
        first = pl.multiple_of(tile * TILE, TILE)
        scale = squares[pl.ds(first, TILE), :]
        for group in range(groups):
            part = summed[pl.ds(first * SUB + group, TILE, stride=SUB), :]
            out_ref[pl.ds(first, TILE), lane_group(group)] = (
                part * scale * gain_ref[:, lane_group(group)]
            ).astype(jnp.bfloat16)

    @pl.when(me < ctx_size - 1)
    def _():
        edge_copy.wait_send()
        product_copy.wait_send()

    for step in range(1, ctx_size):
        @pl.when(me + step < ctx_size)
        def _():
            state_copy(step).wait_send()

    for step in range(1, ch_size):
        sum_copy(step).wait_send()


def on_device(
    ctx_size, ch_size, projected, short_filter, medium_filter, decay, residues, skip_gain, out_gain
):
    rows = projected.shape[1]
    chans = projected.shape[2]
    padded = -(-rows // LANES) * LANES
    f32 = jnp.float32
    bf16 = jnp.bfloat16

    def token_buffer(count, dtype=f32):
        return pltpu.VMEM((count * SUB, LANES), dtype)

    dma = pltpu.SemaphoreType.DMA
    vmem = pl.BlockSpec(memory_space=pltpu.VMEM)
    flops = rows * chans * (2 * MED + 6 * SHORT + 8 * MODES)
    return pl.pallas_call(
        functools.partial(block_kernel, ctx_size, ch_size),
        out_shape=jax.ShapeDtypeStruct((rows, chans), bf16),
        in_specs=[vmem] * 7,
        out_specs=vmem,
        scratch_shapes=[
            token_buffer(LEAD + rows),
            token_buffer(LEAD + rows),
            token_buffer(LEAD + rows),
            token_buffer(SHORT * 3),
            token_buffer(MED),
            token_buffer(MED + rows),
            token_buffer(rows),
            token_buffer(rows),
            token_buffer(rows),
            token_buffer(MODES),
            token_buffer(MODES),
            token_buffer(MODES),
            pltpu.VMEM((padded, LANES), f32),
            pltpu.VMEM((3, TILE, chans), bf16),
            token_buffer(MED, bf16),
            token_buffer(MED, bf16),
            token_buffer(MODES, bf16),
            pltpu.VMEM((ctx_size - 1, MODES * SUB, LANES), bf16),
            pltpu.VMEM((SUB, padded), f32),
            pltpu.VMEM((ch_size - 1, SUB, padded), f32),
            dma((2,)),
            dma((2,)),
            dma((ctx_size - 1,)),
            dma((ctx_size - 1,)),
            dma((ch_size - 1,)),
            dma((ch_size - 1,)),
        ],
        compiler_params=pltpu.CompilerParams(
            collective_id=0, has_side_effects=True, vmem_limit_bytes=40 * 1024 * 1024
        ),
        cost_estimate=pl.CostEstimate(
            flops=flops, bytes_accessed=rows * chans * 8, transcendentals=0
        ),
    )(
        projected,
        short_filter,
        medium_filter,
        decay,
        residues,
        skip_gain.reshape(chans // LANES, LANES),
        out_gain.reshape(1, chans),
    )


def solution(mesh):
    in_specs = (
        P(None, "ctx", "ch"),
        P(None, None, "ch"),
        P(None, "ch"),
        P(None, "ch"),
        P(None, "ch"),
        P("ch"),
        P("ch"),
    )
    out_specs = P("ctx", "ch")
    body = functools.partial(on_device, mesh.shape["ctx"], mesh.shape["ch"])
    return jax.shard_map(
        body, mesh=mesh, in_specs=in_specs, out_specs=out_specs, check_vma=False
    )
```

```python
import functools

import jax
import jax.numpy as jnp
from jax import lax
from jax.experimental import pallas as pl
from jax.experimental.pallas import tpu as pltpu
from jax.sharding import PartitionSpec as P

C = 4096
SHORT = 7
MED = 128
MODES = 16
LANES = 128
SUB = 8
LEAD = 8
TILE = 16
TAPS = 8
norm_eps = 1e-06
MESH = pl.DeviceIdType.MESH


def as_tokens(rows):
    return rows.reshape(rows.shape[0] // SUB, SUB, LANES)


def as_rows(tokens):
    return tokens.reshape(tokens.shape[0] * SUB, LANES)


def token_rows(first, count):
    start = first * SUB
    if not isinstance(start, int):
        start = pl.multiple_of(start, SUB)
    return pl.ds(start, count * SUB)


def rounded(tokens):
    return as_tokens(as_rows(tokens).astype(jnp.bfloat16).astype(jnp.float32))


def mode_sum(parts):
    count = parts.shape[0]
    while count > 1:
        count //= 2
        parts = parts[:count] + parts[count:]
    return parts[0]


def block_kernel(
    ctx_size,
    ch_size,
    proj_hbm,
    short_hbm,
    medium_hbm,
    decay_hbm,
    residue_hbm,
    skip_hbm,
    gain_hbm,
    out_ref,
    proj_ref,
    short_ref,
    medium_ref,
    decay_ref,
    residue_ref,
    skip_ref,
    gain_ref,
    load_sems,
    series0,
    series1,
    series2,
    short_taps,
    medium_taps,
    product,
    queries,
    mediated,
    summed,
    rates,
    weights_buf,
    carry,
    squares,
    edge_recv,
    product_send,
    product_recv,
    state_send,
    state_recv,
    sum_send,
    sum_recv,
    edge_sems,
    product_sems,
    state_send_sems,
    state_recv_sems,
    sum_send_sems,
    sum_recv_sems,
):
    rows = proj_ref.shape[1]
    groups = proj_ref.shape[2] // LANES
    series = (series0, series1, series2)
    me = lax.axis_index("ctx")
    my_ch = lax.axis_index("ch")
    following = lax.rem(me + 1, ctx_size)

    pairs = {
        "short": (short_hbm, short_ref),
        "key": (proj_hbm.at[1], proj_ref.at[1]),
        "value": (proj_hbm.at[2], proj_ref.at[2]),
        "medium": (medium_hbm, medium_ref),
        "query": (proj_hbm.at[0], proj_ref.at[0]),
        "decay": (decay_hbm, decay_ref),
        "residue": (residue_hbm, residue_ref),
        "skip": (skip_hbm, skip_ref),
        "gain": (gain_hbm, gain_ref),
    }
    loads = {
        name: pltpu.make_async_copy(source, target, load_sems.at[position])
        for position, (name, (source, target)) in enumerate(pairs.items())
    }
    for load in loads.values():
        load.start()

    barrier = pltpu.get_barrier_semaphore()
    for step in range(1, ctx_size):
        pl.semaphore_signal(
            barrier,
            inc=1,
            device_id={"ctx": lax.rem(me + step, ctx_size)},
            device_id_type=MESH,
        )
    for step in range(1, ch_size):
        pl.semaphore_signal(
            barrier,
            inc=1,
            device_id={"ch": lax.rem(my_ch + step, ch_size)},
            device_id_type=MESH,
        )

    if groups < SUB:
        for ref in (
            series0, series1, series2, short_taps, medium_taps, rates, weights_buf,
        ):
            ref[...] = jnp.zeros(ref.shape, ref.dtype)

    def lane_group(group):
        return slice(group * LANES, (group + 1) * LANES)

    def spread_series(index):
        @pl.loop(0, rows // TILE)
        def _(tile):
            first = pl.multiple_of(tile * TILE, TILE)
            for group in range(groups):
                part = proj_ref[index, pl.ds(first, TILE), lane_group(group)]
                series[index][
                    pl.ds((LEAD + first) * SUB + group, TILE, stride=SUB), :
                ] = part.astype(jnp.float32)

    loads["short"].wait()
    for index in range(3):
        for group in range(groups):
            short_taps[pl.ds(index * SHORT * SUB + group, SHORT, stride=SUB), :] = short_ref[
                index, :, lane_group(group)
            ]
    loads["key"].wait()
    spread_series(1)
    loads["value"].wait()
    spread_series(2)

    pl.semaphore_wait(barrier, ctx_size - 1 + ch_size - 1)

    edge_copy = pltpu.make_async_remote_copy(
        src_ref=proj_hbm.at[:, pl.ds(rows - TILE, TILE), :],
        dst_ref=edge_recv,
        send_sem=edge_sems.at[0],
        recv_sem=edge_sems.at[1],
        device_id={"ctx": following},
        device_id_type=MESH,
    )
    product_copy = pltpu.make_async_remote_copy(
        src_ref=product_send,
        dst_ref=product_recv,
        send_sem=product_sems.at[0],
        recv_sem=product_sems.at[1],
        device_id={"ctx": following},
        device_id_type=MESH,
    )

    @pl.when(me < ctx_size - 1)
    def _():
        edge_copy.start()

    def featured(index, first):
        window = as_tokens(series[index][token_rows(LEAD + first - (SHORT - 1), TILE + SHORT - 1), :])
        total = None
        for delay in range(SHORT):
            tap = short_taps[(index * SHORT + delay) * SUB : (index * SHORT + delay + 1) * SUB, :]
            offset = SHORT - 1 - delay
            term = tap[None] * window[offset : offset + TILE]
            total = term if total is None else total + term
        return rounded(total)

    def product_tile(first):
        return as_rows(featured(1, first) * featured(2, first)).astype(jnp.bfloat16)

    own_first = rows - MED

    @pl.loop(own_first // TILE, rows // TILE)
    def _(tile):
        first = tile * TILE
        value = product_tile(first)
        product_send[
            pl.ds(pl.multiple_of((first - own_first) * SUB, TILE * SUB), TILE * SUB), :
        ] = value
        product[token_rows(MED + first, TILE), :] = value.astype(jnp.float32)

    @pl.when(me < ctx_size - 1)
    def _():
        product_copy.start()

    loads["medium"].wait()

    @pl.loop(0, MED // TILE)
    def _(tile):
        first = pl.multiple_of(tile * TILE, TILE)
        for group in range(groups):
            part = medium_ref[pl.ds(first, TILE), lane_group(group)]
            medium_taps[pl.ds(first * SUB + group, TILE, stride=SUB), :] = part.astype(jnp.float32)

    loads["query"].wait()
    spread_series(0)

    loads["decay"].wait()
    loads["residue"].wait()
    for group in range(groups):
        rate = decay_ref[:, lane_group(group)]
        twice = 2.0 * rate
        series_form = twice * (
            1.0
            - twice
            * (0.5 - twice * (1.0 / 6.0 - twice * (1.0 / 24.0 - twice * (1.0 / 120.0 - twice / 720.0))))
        )
        power = jnp.where(twice < 0.125, series_form, 1.0 - jnp.exp(-twice))
        rates[pl.ds(group, MODES, stride=SUB), :] = rate
        weights_buf[pl.ds(group, MODES, stride=SUB), :] = residue_ref[
            :, lane_group(group)
        ] * jnp.sqrt(power)

    @pl.when(me > 0)
    def _():
        edge_copy.wait_recv()
        for index in range(3):
            for group in range(groups):
                part = edge_recv[index, :, lane_group(group)].astype(jnp.float32)
                series[index][pl.ds(group, LEAD, stride=SUB), :] = part[TILE - LEAD :]

    @pl.when(me == 0)
    def _():
        for index in range(3):
            series[index][0 : LEAD * SUB, :] = jnp.zeros((LEAD * SUB, LANES), jnp.float32)

    @pl.loop(0, own_first // TILE)
    def _(tile):
        first = tile * TILE
        product[token_rows(MED + first, TILE), :] = product_tile(first).astype(jnp.float32)

    @pl.loop(0, rows // TILE)
    def _(tile):
        first = tile * TILE
        queries[token_rows(first, TILE), :] = as_rows(featured(0, first))

    def medium_tile(tile):
        first = tile * TILE

        def add_taps(step, total):
            delay = step * TAPS
            window = as_tokens(
                product[token_rows(MED + first - delay - (TAPS - 1), TILE + TAPS - 1), :]
            )
            taps = as_tokens(medium_taps[token_rows(delay, TAPS), :])
            for within in range(TAPS):
                offset = TAPS - 1 - within
                total = total + taps[within][None] * window[offset : offset + TILE]
            return total

        total = lax.fori_loop(
            0, MED // TAPS, add_taps, jnp.zeros((TILE, SUB, LANES), jnp.float32)
        )
        mediated[token_rows(first, TILE), :] = as_rows(rounded(total))

    @pl.loop(MED // TILE, rows // TILE)
    def _(tile):
        medium_tile(tile)

    @pl.when(me > 0)
    def _():
        product_copy.wait_recv()

        @pl.loop(0, MED // TILE)
        def _(tile):
            start = pl.multiple_of(tile * TILE * SUB, TILE * SUB)
            part = product_recv[pl.ds(start, TILE * SUB), :]
            product[pl.ds(start, TILE * SUB), :] = part.astype(jnp.float32)

    @pl.when(me == 0)
    def _():
        product[0 : MED * SUB, :] = jnp.zeros((MED * SUB, LANES), jnp.float32)

    @pl.loop(0, MED // TILE)
    def _(tile):
        medium_tile(tile)

    decay_step = jnp.exp(-as_tokens(rates[...]))
    weights = as_tokens(weights_buf[...])

    def state_step(step, state):
        inputs = as_tokens(mediated[token_rows(step * SUB, SUB), :])
        for within in range(SUB):
            state = decay_step * state + inputs[within][None]
        return state

    zero_state = jnp.zeros((MODES, SUB, LANES), jnp.float32)
    final = lax.fori_loop(0, rows // SUB, state_step, zero_state)
    state_send[...] = as_rows(final).astype(jnp.bfloat16)

    def state_copy(step):
        return pltpu.make_async_remote_copy(
            src_ref=state_send,
            dst_ref=state_recv.at[step - 1],
            send_sem=state_send_sems.at[step - 1],
            recv_sem=state_recv_sems.at[step - 1],
            device_id={"ctx": lax.rem(me + step, ctx_size)},
            device_id_type=MESH,
        )

    for step in range(1, ctx_size):
        @pl.when(me + step < ctx_size)
        def _():
            state_copy(step).start()

    loads["skip"].wait()
    loads["gain"].wait()
    skip = skip_ref[...]
    if groups < SUB:
        skip = jnp.concatenate([skip, jnp.zeros((SUB - groups, LANES), jnp.float32)], 0)

    def local_step(step, state):
        inputs = as_tokens(mediated[token_rows(step * SUB, SUB), :])
        sums = []
        for within in range(SUB):
            state = decay_step * state + inputs[within][None]
            sums.append((mode_sum(weights * state) + skip * inputs[within])[None])
        summed[token_rows(step * SUB, SUB), :] = as_rows(jnp.concatenate(sums, 0))
        return state

    lax.fori_loop(0, rows // SUB, local_step, zero_state)

    carry[...] = jnp.zeros(carry.shape, jnp.float32)
    for step in reversed(range(1, ctx_size)):
        @pl.when(me >= step)
        def _():
            state_copy(step).wait_recv()
            span = jnp.exp(-float(rows) * rates[...])
            carry[...] = carry[...] * span + state_recv[step - 1].astype(jnp.float32)

    def carried_step(step, state):
        queried = as_tokens(queries[token_rows(step * SUB, SUB), :])
        local = as_tokens(summed[token_rows(step * SUB, SUB), :])
        gated = []
        for within in range(SUB):
            state = decay_step * state
            gated.append((queried[within] * (local[within] + mode_sum(state)))[None])
        summed[token_rows(step * SUB, SUB), :] = as_rows(jnp.concatenate(gated, 0))
        return state

    lax.fori_loop(0, rows // SUB, carried_step, weights * as_tokens(carry[...]))

    padded = squares.shape[0]
    if padded > rows:
        squares[rows:padded, :] = jnp.zeros((padded - rows, LANES), jnp.float32)

    @pl.loop(0, rows // SUB)
    def _(tile):
        first = pl.multiple_of(tile * SUB, SUB)
        total = None
        for group in range(groups):
            part = summed[pl.ds(first * SUB + group, SUB, stride=SUB), :]
            total = part * part if total is None else total + part * part
        squares[pl.ds(first, SUB), :] = total

    own_sum = lax.dot_general(
        jnp.ones((SUB, LANES), jnp.float32),
        squares[...],
        (((1,), (1,)), ((), ())),
        precision=lax.Precision.HIGHEST,
        preferred_element_type=jnp.float32,
    )
    sum_send[...] = own_sum

    def sum_copy(step):
        return pltpu.make_async_remote_copy(
            src_ref=sum_send,
            dst_ref=sum_recv.at[step - 1],
            send_sem=sum_send_sems.at[step - 1],
            recv_sem=sum_recv_sems.at[step - 1],
            device_id={"ch": lax.rem(my_ch + step, ch_size)},
            device_id_type=MESH,
        )

    for step in range(1, ch_size):
        sum_copy(step).start()
    total_sum = own_sum
    for step in range(1, ch_size):
        sum_copy(step).wait_recv()
        total_sum = total_sum + sum_recv[step - 1]
    inverse = lax.rsqrt(total_sum / C + norm_eps)
    same = lax.broadcasted_iota(jnp.int32, (padded, padded), 0) == lax.broadcasted_iota(
        jnp.int32, (padded, padded), 1
    )
    column = jnp.sum(
        jnp.where(same, jnp.broadcast_to(inverse[0:1], (padded, padded)), 0.0), 1, keepdims=True
    )
    squares[...] = jnp.broadcast_to(column, (padded, LANES))

    @pl.loop(0, rows // TILE)
    def _(tile):
        first = pl.multiple_of(tile * TILE, TILE)
        scale = squares[pl.ds(first, TILE), :]
        for group in range(groups):
            part = summed[pl.ds(first * SUB + group, TILE, stride=SUB), :]
            out_ref[pl.ds(first, TILE), lane_group(group)] = (
                part * scale * gain_ref[:, lane_group(group)]
            ).astype(jnp.bfloat16)

    @pl.when(me < ctx_size - 1)
    def _():
        edge_copy.wait_send()
        product_copy.wait_send()

    for step in range(1, ctx_size):
        @pl.when(me + step < ctx_size)
        def _():
            state_copy(step).wait_send()

    for step in range(1, ch_size):
        sum_copy(step).wait_send()


def on_device(
    ctx_size, ch_size, projected, short_filter, medium_filter, decay, residues, skip_gain, out_gain
):
    rows = projected.shape[1]
    chans = projected.shape[2]
    padded = -(-rows // LANES) * LANES
    f32 = jnp.float32
    bf16 = jnp.bfloat16

    def token_buffer(count, dtype=f32):
        return pltpu.VMEM((count * SUB, LANES), dtype)

    dma = pltpu.SemaphoreType.DMA
    vmem = pl.BlockSpec(memory_space=pltpu.VMEM)
    flops = rows * chans * (2 * MED + 6 * SHORT + 8 * MODES)
    return pl.pallas_call(
        functools.partial(block_kernel, ctx_size, ch_size),
        out_shape=jax.ShapeDtypeStruct((rows, chans), bf16),
        in_specs=[pl.BlockSpec(memory_space=pltpu.HBM)] * 7,
        out_specs=vmem,
        scratch_shapes=[
            pltpu.VMEM(projected.shape, bf16),
            pltpu.VMEM((3, SHORT, chans), f32),
            pltpu.VMEM(medium_filter.shape, bf16),
            pltpu.VMEM(decay.shape, f32),
            pltpu.VMEM(residues.shape, f32),
            pltpu.VMEM((chans // LANES, LANES), f32),
            pltpu.VMEM((1, chans), f32),
            dma((9,)),
            token_buffer(LEAD + rows),
            token_buffer(LEAD + rows),
            token_buffer(LEAD + rows),
            token_buffer(SHORT * 3),
            token_buffer(MED),
            token_buffer(MED + rows),
            token_buffer(rows),
            token_buffer(rows),
            token_buffer(rows),
            token_buffer(MODES),
            token_buffer(MODES),
            token_buffer(MODES),
            pltpu.VMEM((padded, LANES), f32),
            pltpu.VMEM((3, TILE, chans), bf16),
            token_buffer(MED, bf16),
            token_buffer(MED, bf16),
            token_buffer(MODES, bf16),
            pltpu.VMEM((ctx_size - 1, MODES * SUB, LANES), bf16),
            pltpu.VMEM((SUB, padded), f32),
            pltpu.VMEM((ch_size - 1, SUB, padded), f32),
            dma((2,)),
            dma((2,)),
            dma((ctx_size - 1,)),
            dma((ctx_size - 1,)),
            dma((ch_size - 1,)),
            dma((ch_size - 1,)),
        ],
        compiler_params=pltpu.CompilerParams(
            collective_id=0, has_side_effects=True, vmem_limit_bytes=63 * 1024 * 1024
        ),
        cost_estimate=pl.CostEstimate(
            flops=flops, bytes_accessed=rows * chans * 8, transcendentals=0
        ),
    )(
        projected,
        jnp.transpose(short_filter, (1, 0, 2)),
        medium_filter,
        decay,
        residues,
        skip_gain.reshape(chans // LANES, LANES),
        out_gain.reshape(1, chans),
    )


def solution(mesh):
    in_specs = (
        P(None, "ctx", "ch"),
        P(None, None, "ch"),
        P(None, "ch"),
        P(None, "ch"),
        P(None, "ch"),
        P("ch"),
        P("ch"),
    )
    out_specs = P("ctx", "ch")
    body = functools.partial(on_device, mesh.shape["ctx"], mesh.shape["ch"])
    return jax.shard_map(
        body, mesh=mesh, in_specs=in_specs, out_specs=out_specs, check_vma=False
    )
```

```python
import functools

import jax
import jax.numpy as jnp
from jax import lax
from jax.experimental import pallas as pl
from jax.experimental.pallas import tpu as pltpu
from jax.sharding import PartitionSpec as P

C = 4096
SHORT = 7
MED = 128
MODES = 16
LANES = 128
SUB = 8
LEAD = 8
TILE = 16
GROUP = 16
PAIRS = 4
PAD = 1
norm_eps = 1e-06
MESH = pl.DeviceIdType.MESH


def as_tokens(rows):
    return rows.reshape(rows.shape[0] // SUB, SUB, LANES)


def as_rows(tokens):
    return tokens.reshape(tokens.shape[0] * SUB, LANES)


def token_rows(first, count):
    start = first * SUB
    if not isinstance(start, int):
        start = pl.multiple_of(start, SUB)
    return pl.ds(start, count * SUB)


def as_pairs(rows):
    return rows.reshape(rows.shape[0] // (2 * SUB), 2 * SUB, LANES)


def rounded(tokens):
    return as_tokens(as_rows(tokens).astype(jnp.bfloat16).astype(jnp.float32))


def mode_sum(parts):
    count = parts.shape[0]
    while count > 1:
        count //= 2
        parts = parts[:count] + parts[count:]
    return parts[0]


def block_kernel(
    ctx_size,
    ch_size,
    proj_hbm,
    short_hbm,
    medium_hbm,
    decay_hbm,
    residue_hbm,
    skip_hbm,
    gain_hbm,
    out_ref,
    proj_ref,
    short_ref,
    medium_ref,
    decay_ref,
    residue_ref,
    skip_ref,
    gain_ref,
    load_sems,
    series0,
    series1,
    series2,
    short_taps,
    medium_taps,
    pair_taps,
    even_pairs,
    odd_pairs,
    product,
    queries,
    mediated,
    summed,
    rates,
    weights_buf,
    carry,
    squares,
    edge_recv,
    product_send,
    product_recv,
    state_send,
    state_recv,
    sum_send,
    sum_recv,
    edge_sems,
    product_sems,
    state_send_sems,
    state_recv_sems,
    sum_send_sems,
    sum_recv_sems,
):
    rows = proj_ref.shape[1]
    groups = proj_ref.shape[2] // LANES
    series = (series0, series1, series2)
    me = lax.axis_index("ctx")
    my_ch = lax.axis_index("ch")
    following = lax.rem(me + 1, ctx_size)

    pairs = {
        "short": (short_hbm, short_ref),
        "key": (proj_hbm.at[1], proj_ref.at[1]),
        "value": (proj_hbm.at[2], proj_ref.at[2]),
        "medium": (medium_hbm, medium_ref),
        "query": (proj_hbm.at[0], proj_ref.at[0]),
        "decay": (decay_hbm, decay_ref),
        "residue": (residue_hbm, residue_ref),
        "skip": (skip_hbm, skip_ref),
        "gain": (gain_hbm, gain_ref),
    }
    loads = {
        name: pltpu.make_async_copy(source, target, load_sems.at[position])
        for position, (name, (source, target)) in enumerate(pairs.items())
    }
    for load in loads.values():
        load.start()

    barrier = pltpu.get_barrier_semaphore()
    for step in range(1, ctx_size):
        pl.semaphore_signal(
            barrier,
            inc=1,
            device_id={"ctx": lax.rem(me + step, ctx_size)},
            device_id_type=MESH,
        )
    for step in range(1, ch_size):
        pl.semaphore_signal(
            barrier,
            inc=1,
            device_id={"ch": lax.rem(my_ch + step, ch_size)},
            device_id_type=MESH,
        )

    if groups < SUB:
        for ref in (
            series0, series1, series2, short_taps, medium_taps, rates, weights_buf,
        ):
            ref[...] = jnp.zeros(ref.shape, ref.dtype)

    def lane_group(group):
        return slice(group * LANES, (group + 1) * LANES)

    def spread_series(index):
        @pl.loop(0, rows // TILE)
        def _(tile):
            first = pl.multiple_of(tile * TILE, TILE)
            for group in range(groups):
                part = proj_ref[index, pl.ds(first, TILE), lane_group(group)]
                series[index][
                    pl.ds((LEAD + first) * SUB + group, TILE, stride=SUB), :
                ] = part.astype(jnp.float32)

    loads["short"].wait()
    for index in range(3):
        for group in range(groups):
            short_taps[pl.ds(index * SHORT * SUB + group, SHORT, stride=SUB), :] = short_ref[
                index, :, lane_group(group)
            ]
    loads["key"].wait()
    spread_series(1)
    loads["value"].wait()
    spread_series(2)

    pl.semaphore_wait(barrier, ctx_size - 1 + ch_size - 1)

    edge_copy = pltpu.make_async_remote_copy(
        src_ref=proj_hbm.at[:, pl.ds(rows - TILE, TILE), :],
        dst_ref=edge_recv,
        send_sem=edge_sems.at[0],
        recv_sem=edge_sems.at[1],
        device_id={"ctx": following},
        device_id_type=MESH,
    )
    product_copy = pltpu.make_async_remote_copy(
        src_ref=product_send,
        dst_ref=product_recv,
        send_sem=product_sems.at[0],
        recv_sem=product_sems.at[1],
        device_id={"ctx": following},
        device_id_type=MESH,
    )

    @pl.when(me < ctx_size - 1)
    def _():
        edge_copy.start()

    def featured(index, first):
        window = as_tokens(series[index][token_rows(LEAD + first - (SHORT - 1), TILE + SHORT - 1), :])
        total = None
        for delay in range(SHORT):
            tap = short_taps[(index * SHORT + delay) * SUB : (index * SHORT + delay + 1) * SUB, :]
            offset = SHORT - 1 - delay
            term = tap[None] * window[offset : offset + TILE]
            total = term if total is None else total + term
        return rounded(total)

    def product_tile(first):
        return as_rows(featured(1, first) * featured(2, first)).astype(jnp.bfloat16)

    def keep_product(tile, value):
        product[token_rows(PAD + MED + tile * TILE, TILE), :] = value.astype(jnp.float32)
        even_pairs[pl.ds(MED // 2 + tile * (TILE // 2), TILE // 2)] = as_pairs(value)

    own_first = rows - MED
    product[0 : PAD * SUB, :] = jnp.zeros((PAD * SUB, LANES), jnp.float32)

    @pl.loop(own_first // TILE, rows // TILE)
    def _(tile):
        first = tile * TILE
        value = product_tile(first)
        product_send[
            pl.ds(pl.multiple_of((first - own_first) * SUB, TILE * SUB), TILE * SUB), :
        ] = value
        keep_product(tile, value)

    @pl.when(me < ctx_size - 1)
    def _():
        product_copy.start()

    loads["medium"].wait()

    @pl.loop(0, MED // TILE)
    def _(tile):
        first = pl.multiple_of(tile * TILE, TILE)
        for group in range(groups):
            part = medium_ref[pl.ds(first, TILE), lane_group(group)]
            medium_taps[pl.ds(first * SUB + group, TILE, stride=SUB), :] = part.astype(jnp.float32)
        taps = as_tokens(medium_taps[token_rows(first, TILE), :])
        pair_taps[pl.ds(first, TILE)] = jnp.concatenate([taps, taps], 1).astype(jnp.bfloat16)

    loads["query"].wait()
    spread_series(0)

    loads["decay"].wait()
    loads["residue"].wait()
    for group in range(groups):
        rate = decay_ref[:, lane_group(group)]
        twice = 2.0 * rate
        series_form = twice * (
            1.0
            - twice
            * (0.5 - twice * (1.0 / 6.0 - twice * (1.0 / 24.0 - twice * (1.0 / 120.0 - twice / 720.0))))
        )
        power = jnp.where(twice < 0.125, series_form, 1.0 - jnp.exp(-twice))
        rates[pl.ds(group, MODES, stride=SUB), :] = rate
        weights_buf[pl.ds(group, MODES, stride=SUB), :] = residue_ref[
            :, lane_group(group)
        ] * jnp.sqrt(power)

    @pl.when(me > 0)
    def _():
        edge_copy.wait_recv()
        for index in range(3):
            for group in range(groups):
                part = edge_recv[index, :, lane_group(group)].astype(jnp.float32)
                series[index][pl.ds(group, LEAD, stride=SUB), :] = part[TILE - LEAD :]

    @pl.when(me == 0)
    def _():
        for index in range(3):
            series[index][0 : LEAD * SUB, :] = jnp.zeros((LEAD * SUB, LANES), jnp.float32)

    @pl.loop(0, own_first // TILE)
    def _(tile):
        keep_product(tile, product_tile(tile * TILE))

    @pl.loop(0, rows // TILE)
    def _(tile):
        first = tile * TILE
        queries[token_rows(first, TILE), :] = as_rows(featured(0, first))

    def shift_tile(tile):
        first = tile * TILE
        part = product[token_rows(first, TILE), :]
        odd_pairs[pl.ds(tile * (TILE // 2), TILE // 2)] = as_pairs(part.astype(jnp.bfloat16))

    def medium_tile(tile):
        first_pair = tile * PAIRS
        total = None
        for delay in range(0, MED, GROUP):
            start = (MED - delay - GROUP) // 2 + 1 + first_pair
            even = even_pairs[pl.ds(start, PAIRS + GROUP // 2 - 1)]
            odd = odd_pairs[pl.ds(start, PAIRS + GROUP // 2 - 1)]
            terms = []
            for within in range(GROUP):
                window = odd if within % 2 else even
                offset = GROUP // 2 - 1 - within // 2
                terms.append(pair_taps[delay + within][None] * window[offset : offset + PAIRS])
            while len(terms) > 1:
                terms = [left + right for left, right in zip(terms[::2], terms[1::2])]
            part = terms[0].astype(jnp.float32)
            total = part if total is None else total + part
        value = total.astype(jnp.bfloat16).astype(jnp.float32)
        mediated[token_rows(first_pair * 2, PAIRS * 2), :] = value.reshape(PAIRS * 2 * SUB, LANES)

    @pl.loop(MED // TILE, (MED + rows) // TILE)
    def _(tile):
        shift_tile(tile)

    @pl.loop(MED // (2 * PAIRS), rows // (2 * PAIRS))
    def _(tile):
        medium_tile(tile)

    @pl.when(me > 0)
    def _():
        product_copy.wait_recv()

        @pl.loop(0, MED // TILE)
        def _(tile):
            start = pl.multiple_of(tile * TILE * SUB, TILE * SUB)
            part = product_recv[pl.ds(start, TILE * SUB), :]
            product[token_rows(PAD + tile * TILE, TILE), :] = part.astype(jnp.float32)
            even_pairs[pl.ds(tile * (TILE // 2), TILE // 2)] = as_pairs(part)

    @pl.when(me == 0)
    def _():
        product[PAD * SUB : (PAD + MED) * SUB, :] = jnp.zeros((MED * SUB, LANES), jnp.float32)
        even_pairs[0 : MED // 2] = jnp.zeros((MED // 2, 2 * SUB, LANES), jnp.bfloat16)

    @pl.loop(0, MED // TILE + 1)
    def _(tile):
        shift_tile(tile)

    @pl.loop(0, MED // (2 * PAIRS))
    def _(tile):
        medium_tile(tile)

    decay_step = jnp.exp(-as_tokens(rates[...]))
    weights = as_tokens(weights_buf[...])

    def state_step(step, state):
        inputs = as_tokens(mediated[token_rows(step * SUB, SUB), :])
        for within in range(SUB):
            state = decay_step * state + inputs[within][None]
        return state

    zero_state = jnp.zeros((MODES, SUB, LANES), jnp.float32)
    final = lax.fori_loop(0, rows // SUB, state_step, zero_state)
    state_send[...] = as_rows(final).astype(jnp.bfloat16)

    def state_copy(step):
        return pltpu.make_async_remote_copy(
            src_ref=state_send,
            dst_ref=state_recv.at[step - 1],
            send_sem=state_send_sems.at[step - 1],
            recv_sem=state_recv_sems.at[step - 1],
            device_id={"ctx": lax.rem(me + step, ctx_size)},
            device_id_type=MESH,
        )

    for step in range(1, ctx_size):
        @pl.when(me + step < ctx_size)
        def _():
            state_copy(step).start()

    loads["skip"].wait()
    loads["gain"].wait()
    skip = skip_ref[...]
    if groups < SUB:
        skip = jnp.concatenate([skip, jnp.zeros((SUB - groups, LANES), jnp.float32)], 0)

    def local_step(step, state):
        inputs = as_tokens(mediated[token_rows(step * SUB, SUB), :])
        sums = []
        for within in range(SUB):
            state = decay_step * state + inputs[within][None]
            sums.append((mode_sum(weights * state) + skip * inputs[within])[None])
        summed[token_rows(step * SUB, SUB), :] = as_rows(jnp.concatenate(sums, 0))
        return state

    lax.fori_loop(0, rows // SUB, local_step, zero_state)

    carry[...] = jnp.zeros(carry.shape, jnp.float32)
    for step in reversed(range(1, ctx_size)):
        @pl.when(me >= step)
        def _():
            state_copy(step).wait_recv()
            span = jnp.exp(-float(rows) * rates[...])
            carry[...] = carry[...] * span + state_recv[step - 1].astype(jnp.float32)

    def carried_step(step, state):
        queried = as_tokens(queries[token_rows(step * SUB, SUB), :])
        local = as_tokens(summed[token_rows(step * SUB, SUB), :])
        gated = []
        for within in range(SUB):
            state = decay_step * state
            gated.append((queried[within] * (local[within] + mode_sum(state)))[None])
        summed[token_rows(step * SUB, SUB), :] = as_rows(jnp.concatenate(gated, 0))
        return state

    lax.fori_loop(0, rows // SUB, carried_step, weights * as_tokens(carry[...]))

    padded = squares.shape[0]
    if padded > rows:
        squares[rows:padded, :] = jnp.zeros((padded - rows, LANES), jnp.float32)

    @pl.loop(0, rows // SUB)
    def _(tile):
        first = pl.multiple_of(tile * SUB, SUB)
        total = None
        for group in range(groups):
            part = summed[pl.ds(first * SUB + group, SUB, stride=SUB), :]
            total = part * part if total is None else total + part * part
        squares[pl.ds(first, SUB), :] = total

    own_sum = lax.dot_general(
        jnp.ones((SUB, LANES), jnp.float32),
        squares[...],
        (((1,), (1,)), ((), ())),
        precision=lax.Precision.HIGHEST,
        preferred_element_type=jnp.float32,
    )
    sum_send[...] = own_sum

    def sum_copy(step):
        return pltpu.make_async_remote_copy(
            src_ref=sum_send,
            dst_ref=sum_recv.at[step - 1],
            send_sem=sum_send_sems.at[step - 1],
            recv_sem=sum_recv_sems.at[step - 1],
            device_id={"ch": lax.rem(my_ch + step, ch_size)},
            device_id_type=MESH,
        )

    for step in range(1, ch_size):
        sum_copy(step).start()
    total_sum = own_sum
    for step in range(1, ch_size):
        sum_copy(step).wait_recv()
        total_sum = total_sum + sum_recv[step - 1]
    inverse = lax.rsqrt(total_sum / C + norm_eps)
    same = lax.broadcasted_iota(jnp.int32, (padded, padded), 0) == lax.broadcasted_iota(
        jnp.int32, (padded, padded), 1
    )
    column = jnp.sum(
        jnp.where(same, jnp.broadcast_to(inverse[0:1], (padded, padded)), 0.0), 1, keepdims=True
    )
    squares[...] = jnp.broadcast_to(column, (padded, LANES))

    @pl.loop(0, rows // TILE)
    def _(tile):
        first = pl.multiple_of(tile * TILE, TILE)
        scale = squares[pl.ds(first, TILE), :]
        for group in range(groups):
            part = summed[pl.ds(first * SUB + group, TILE, stride=SUB), :]
            out_ref[pl.ds(first, TILE), lane_group(group)] = (
                part * scale * gain_ref[:, lane_group(group)]
            ).astype(jnp.bfloat16)

    @pl.when(me < ctx_size - 1)
    def _():
        edge_copy.wait_send()
        product_copy.wait_send()

    for step in range(1, ctx_size):
        @pl.when(me + step < ctx_size)
        def _():
            state_copy(step).wait_send()

    for step in range(1, ch_size):
        sum_copy(step).wait_send()


def on_device(
    ctx_size, ch_size, projected, short_filter, medium_filter, decay, residues, skip_gain, out_gain
):
    rows = projected.shape[1]
    chans = projected.shape[2]
    padded = -(-rows // LANES) * LANES
    f32 = jnp.float32
    bf16 = jnp.bfloat16

    def token_buffer(count, dtype=f32):
        return pltpu.VMEM((count * SUB, LANES), dtype)

    dma = pltpu.SemaphoreType.DMA
    vmem = pl.BlockSpec(memory_space=pltpu.VMEM)
    flops = rows * chans * (2 * MED + 6 * SHORT + 8 * MODES)
    return pl.pallas_call(
        functools.partial(block_kernel, ctx_size, ch_size),
        out_shape=jax.ShapeDtypeStruct((rows, chans), bf16),
        in_specs=[pl.BlockSpec(memory_space=pltpu.HBM)] * 7,
        out_specs=vmem,
        scratch_shapes=[
            pltpu.VMEM(projected.shape, bf16),
            pltpu.VMEM((3, SHORT, chans), f32),
            pltpu.VMEM(medium_filter.shape, bf16),
            pltpu.VMEM(decay.shape, f32),
            pltpu.VMEM(residues.shape, f32),
            pltpu.VMEM((chans // LANES, LANES), f32),
            pltpu.VMEM((1, chans), f32),
            dma((9,)),
            token_buffer(LEAD + rows),
            token_buffer(LEAD + rows),
            token_buffer(LEAD + rows),
            token_buffer(SHORT * 3),
            token_buffer(MED),
            pltpu.VMEM((MED, 2 * SUB, LANES), bf16),
            pltpu.VMEM(((MED + rows) // 2, 2 * SUB, LANES), bf16),
            pltpu.VMEM(((MED + rows) // 2, 2 * SUB, LANES), bf16),
            token_buffer(PAD + MED + rows),
            token_buffer(rows),
            token_buffer(rows),
            token_buffer(rows),
            token_buffer(MODES),
            token_buffer(MODES),
            token_buffer(MODES),
            pltpu.VMEM((padded, LANES), f32),
            pltpu.VMEM((3, TILE, chans), bf16),
            token_buffer(MED, bf16),
            token_buffer(MED, bf16),
            token_buffer(MODES, bf16),
            pltpu.VMEM((ctx_size - 1, MODES * SUB, LANES), bf16),
            pltpu.VMEM((SUB, padded), f32),
            pltpu.VMEM((ch_size - 1, SUB, padded), f32),
            dma((2,)),
            dma((2,)),
            dma((ctx_size - 1,)),
            dma((ctx_size - 1,)),
            dma((ch_size - 1,)),
            dma((ch_size - 1,)),
        ],
        compiler_params=pltpu.CompilerParams(
            collective_id=0, has_side_effects=True, vmem_limit_bytes=63 * 1024 * 1024
        ),
        cost_estimate=pl.CostEstimate(
            flops=flops, bytes_accessed=rows * chans * 8, transcendentals=0
        ),
    )(
        projected,
        jnp.transpose(short_filter, (1, 0, 2)),
        medium_filter,
        decay,
        residues,
        skip_gain.reshape(chans // LANES, LANES),
        out_gain.reshape(1, chans),
    )


def solution(mesh):
    in_specs = (
        P(None, "ctx", "ch"),
        P(None, None, "ch"),
        P(None, "ch"),
        P(None, "ch"),
        P(None, "ch"),
        P("ch"),
        P("ch"),
    )
    out_specs = P("ctx", "ch")
    body = functools.partial(on_device, mesh.shape["ctx"], mesh.shape["ch"])
    return jax.shard_map(
        body, mesh=mesh, in_specs=in_specs, out_specs=out_specs, check_vma=False
    )
```

```python
import functools

import jax
import jax.numpy as jnp
from jax import lax
from jax.experimental import pallas as pl
from jax.experimental.pallas import tpu as pltpu
from jax.sharding import PartitionSpec as P

C = 4096
SHORT = 7
MED = 128
MODES = 16
LANES = 128
SUB = 8
LEAD = 8
TILE = 16
TAPS = 8
PHASES = 4
SUBS = 9
DEPTH = MED // PHASES
norm_eps = 1e-06
MESH = pl.DeviceIdType.MESH


def as_tokens(rows):
    return rows.reshape(rows.shape[0] // SUB, SUB, LANES)


def as_rows(tokens):
    return tokens.reshape(tokens.shape[0] * SUB, LANES)


def token_rows(first, count):
    start = first * SUB
    if not isinstance(start, int):
        start = pl.multiple_of(start, SUB)
    return pl.ds(start, count * SUB)


def phase_parts(tokens):
    quads = tokens.reshape(tokens.shape[0] // PHASES, PHASES, SUB, LANES)
    part00, part10, part01, part11 = (quads[:, phase] for phase in range(PHASES))
    low, high = part00 + part10, part01 + part11
    parts = (
        part00, part01, part00 + part01,
        part10, part11, part10 + part11,
        low, high, low + high,
    )
    return [as_rows(part) for part in parts]


def rounded(tokens):
    return as_tokens(as_rows(tokens).astype(jnp.bfloat16).astype(jnp.float32))


def mode_sum(parts):
    count = parts.shape[0]
    while count > 1:
        count //= 2
        parts = parts[:count] + parts[count:]
    return parts[0]


def block_kernel(
    ctx_size,
    ch_size,
    proj_hbm,
    short_hbm,
    medium_hbm,
    decay_hbm,
    residue_hbm,
    skip_hbm,
    gain_hbm,
    out_ref,
    proj_ref,
    short_ref,
    medium_ref,
    decay_ref,
    residue_ref,
    skip_ref,
    gain_ref,
    load_sems,
    series0,
    series1,
    series2,
    short_taps,
    medium_taps,
    phased,
    phased_taps,
    filtered,
    queries,
    mediated,
    summed,
    rates,
    weights_buf,
    carry,
    squares,
    edge_recv,
    product_send,
    product_recv,
    state_send,
    state_recv,
    sum_send,
    sum_recv,
    edge_sems,
    product_sems,
    state_send_sems,
    state_recv_sems,
    sum_send_sems,
    sum_recv_sems,
):
    rows = proj_ref.shape[1]
    groups = proj_ref.shape[2] // LANES
    series = (series0, series1, series2)
    me = lax.axis_index("ctx")
    my_ch = lax.axis_index("ch")
    following = lax.rem(me + 1, ctx_size)

    pairs = {
        "short": (short_hbm, short_ref),
        "key": (proj_hbm.at[1], proj_ref.at[1]),
        "value": (proj_hbm.at[2], proj_ref.at[2]),
        "medium": (medium_hbm, medium_ref),
        "query": (proj_hbm.at[0], proj_ref.at[0]),
        "decay": (decay_hbm, decay_ref),
        "residue": (residue_hbm, residue_ref),
        "skip": (skip_hbm, skip_ref),
        "gain": (gain_hbm, gain_ref),
    }
    loads = {
        name: pltpu.make_async_copy(source, target, load_sems.at[position])
        for position, (name, (source, target)) in enumerate(pairs.items())
    }
    for load in loads.values():
        load.start()

    barrier = pltpu.get_barrier_semaphore()
    for step in range(1, ctx_size):
        pl.semaphore_signal(
            barrier,
            inc=1,
            device_id={"ctx": lax.rem(me + step, ctx_size)},
            device_id_type=MESH,
        )
    for step in range(1, ch_size):
        pl.semaphore_signal(
            barrier,
            inc=1,
            device_id={"ch": lax.rem(my_ch + step, ch_size)},
            device_id_type=MESH,
        )

    if groups < SUB:
        for ref in (
            series0, series1, series2, short_taps, medium_taps, rates, weights_buf,
        ):
            ref[...] = jnp.zeros(ref.shape, ref.dtype)

    def lane_group(group):
        return slice(group * LANES, (group + 1) * LANES)

    def spread_series(index):
        @pl.loop(0, rows // TILE)
        def _(tile):
            first = pl.multiple_of(tile * TILE, TILE)
            for group in range(groups):
                part = proj_ref[index, pl.ds(first, TILE), lane_group(group)]
                series[index][
                    pl.ds((LEAD + first) * SUB + group, TILE, stride=SUB), :
                ] = part.astype(jnp.float32)

    loads["short"].wait()
    for index in range(3):
        for group in range(groups):
            short_taps[pl.ds(index * SHORT * SUB + group, SHORT, stride=SUB), :] = short_ref[
                index, :, lane_group(group)
            ]
    loads["key"].wait()
    spread_series(1)
    loads["value"].wait()
    spread_series(2)

    pl.semaphore_wait(barrier, ctx_size - 1 + ch_size - 1)

    edge_copy = pltpu.make_async_remote_copy(
        src_ref=proj_hbm.at[:, pl.ds(rows - TILE, TILE), :],
        dst_ref=edge_recv,
        send_sem=edge_sems.at[0],
        recv_sem=edge_sems.at[1],
        device_id={"ctx": following},
        device_id_type=MESH,
    )
    product_copy = pltpu.make_async_remote_copy(
        src_ref=product_send,
        dst_ref=product_recv,
        send_sem=product_sems.at[0],
        recv_sem=product_sems.at[1],
        device_id={"ctx": following},
        device_id_type=MESH,
    )

    @pl.when(me < ctx_size - 1)
    def _():
        edge_copy.start()

    def featured(index, first):
        window = as_tokens(series[index][token_rows(LEAD + first - (SHORT - 1), TILE + SHORT - 1), :])
        total = None
        for delay in range(SHORT):
            tap = short_taps[(index * SHORT + delay) * SUB : (index * SHORT + delay + 1) * SUB, :]
            offset = SHORT - 1 - delay
            term = tap[None] * window[offset : offset + TILE]
            total = term if total is None else total + term
        return rounded(total)

    def product_tile(first):
        return as_rows(featured(1, first) * featured(2, first)).astype(jnp.bfloat16)

    def keep_product(first, tokens):
        start = pl.multiple_of(first * (SUB // PHASES), TILE * SUB // PHASES)
        for sub, part in enumerate(phase_parts(tokens)):
            phased[sub, pl.ds(start, TILE * SUB // PHASES), :] = part

    own_first = rows - MED

    @pl.loop(own_first // TILE, rows // TILE)
    def _(tile):
        first = tile * TILE
        value = product_tile(first)
        product_send[
            pl.ds(pl.multiple_of((first - own_first) * SUB, TILE * SUB), TILE * SUB), :
        ] = value
        keep_product(MED + first, as_tokens(value.astype(jnp.float32)))

    @pl.when(me < ctx_size - 1)
    def _():
        product_copy.start()

    loads["medium"].wait()

    @pl.loop(0, MED // TILE)
    def _(tile):
        first = pl.multiple_of(tile * TILE, TILE)
        for group in range(groups):
            part = medium_ref[pl.ds(first, TILE), lane_group(group)]
            medium_taps[pl.ds(first * SUB + group, TILE, stride=SUB), :] = part.astype(jnp.float32)
        start = pl.multiple_of(tile * (TILE * SUB // PHASES), TILE * SUB // PHASES)
        taps = as_tokens(medium_taps[token_rows(first, TILE), :])
        for sub, part in enumerate(phase_parts(taps)):
            phased_taps[sub, pl.ds(start, TILE * SUB // PHASES), :] = part

    loads["query"].wait()
    spread_series(0)

    loads["decay"].wait()
    loads["residue"].wait()
    for group in range(groups):
        rate = decay_ref[:, lane_group(group)]
        twice = 2.0 * rate
        series_form = twice * (
            1.0
            - twice
            * (0.5 - twice * (1.0 / 6.0 - twice * (1.0 / 24.0 - twice * (1.0 / 120.0 - twice / 720.0))))
        )
        power = jnp.where(twice < 0.125, series_form, 1.0 - jnp.exp(-twice))
        rates[pl.ds(group, MODES, stride=SUB), :] = rate
        weights_buf[pl.ds(group, MODES, stride=SUB), :] = residue_ref[
            :, lane_group(group)
        ] * jnp.sqrt(power)

    @pl.when(me > 0)
    def _():
        edge_copy.wait_recv()
        for index in range(3):
            for group in range(groups):
                part = edge_recv[index, :, lane_group(group)].astype(jnp.float32)
                series[index][pl.ds(group, LEAD, stride=SUB), :] = part[TILE - LEAD :]

    @pl.when(me == 0)
    def _():
        for index in range(3):
            series[index][0 : LEAD * SUB, :] = jnp.zeros((LEAD * SUB, LANES), jnp.float32)

    @pl.loop(0, own_first // TILE)
    def _(tile):
        first = tile * TILE
        keep_product(MED + first, as_tokens(product_tile(first).astype(jnp.float32)))

    @pl.loop(0, rows // TILE)
    def _(tile):
        first = tile * TILE
        queries[token_rows(first, TILE), :] = as_rows(featured(0, first))

    steps = rows // PHASES

    def sub_filter(sub, first, count):
        total = jnp.zeros((count, SUB, LANES), jnp.float32)
        for delay in range(0, DEPTH, TAPS):
            window = as_tokens(
                phased[sub, token_rows(DEPTH + first - delay - (TAPS - 1), count + TAPS - 1), :]
            )
            taps = as_tokens(phased_taps[sub, token_rows(delay, TAPS), :])
            for within in range(TAPS):
                offset = TAPS - 1 - within
                total = total + taps[within][None] * window[offset : offset + count]
        filtered[sub, token_rows(1 + first, count), :] = as_rows(total)

    def medium_tile(tile):
        @pl.loop(0, SUBS)
        def _(sub):
            sub_filter(sub, tile * TILE, TILE)

    def merge_tile(tile):
        count = TILE // PHASES
        first = tile * count
        wide = [
            as_tokens(filtered[sub, token_rows(first, count + 1), :]) for sub in range(SUBS)
        ]

        def half_rate(base):
            low, high, both = wide[base : base + 3]
            return low[1:] + high[:count], both - low - high

        even0, even1 = half_rate(0)
        odd0, odd1 = half_rate(3)
        both0, both1 = half_rate(6)
        outs = (
            even0 + odd1[:count],
            both0 - even0 - odd0,
            even1[1:] + odd0,
            (both1 - even1 - odd1)[1:],
        )
        tokens = jnp.stack(outs, 1).reshape(TILE, SUB, LANES)
        mediated[token_rows(tile * TILE, TILE), :] = as_rows(rounded(tokens))

    @pl.loop(DEPTH // TILE, steps // TILE)
    def _(tile):
        medium_tile(tile)

    @pl.when(me > 0)
    def _():
        product_copy.wait_recv()

        @pl.loop(0, MED // TILE)
        def _(tile):
            start = pl.multiple_of(tile * TILE * SUB, TILE * SUB)
            part = product_recv[pl.ds(start, TILE * SUB), :]
            keep_product(tile * TILE, as_tokens(part.astype(jnp.float32)))

    @pl.when(me == 0)
    def _():
        phased[:, 0 : DEPTH * SUB, :] = jnp.zeros((SUBS, DEPTH * SUB, LANES), jnp.float32)

    @pl.loop(0, DEPTH // TILE)
    def _(tile):
        medium_tile(tile)

    @pl.loop(0, SUBS)
    def _(sub):
        sub_filter(sub, -1, 1)

    @pl.loop(0, rows // TILE)
    def _(tile):
        merge_tile(tile)

    decay_step = jnp.exp(-as_tokens(rates[...]))
    weights = as_tokens(weights_buf[...])

    def state_step(step, state):
        inputs = as_tokens(mediated[token_rows(step * SUB, SUB), :])
        for within in range(SUB):
            state = decay_step * state + inputs[within][None]
        return state

    zero_state = jnp.zeros((MODES, SUB, LANES), jnp.float32)
    final = lax.fori_loop(0, rows // SUB, state_step, zero_state)
    state_send[...] = as_rows(final).astype(jnp.bfloat16)

    def state_copy(step):
        return pltpu.make_async_remote_copy(
            src_ref=state_send,
            dst_ref=state_recv.at[step - 1],
            send_sem=state_send_sems.at[step - 1],
            recv_sem=state_recv_sems.at[step - 1],
            device_id={"ctx": lax.rem(me + step, ctx_size)},
            device_id_type=MESH,
        )

    for step in range(1, ctx_size):
        @pl.when(me + step < ctx_size)
        def _():
            state_copy(step).start()

    loads["skip"].wait()
    loads["gain"].wait()
    skip = skip_ref[...]
    if groups < SUB:
        skip = jnp.concatenate([skip, jnp.zeros((SUB - groups, LANES), jnp.float32)], 0)

    def local_step(step, state):
        inputs = as_tokens(mediated[token_rows(step * SUB, SUB), :])
        sums = []
        for within in range(SUB):
            state = decay_step * state + inputs[within][None]
            sums.append((mode_sum(weights * state) + skip * inputs[within])[None])
        summed[token_rows(step * SUB, SUB), :] = as_rows(jnp.concatenate(sums, 0))
        return state

    lax.fori_loop(0, rows // SUB, local_step, zero_state)

    carry[...] = jnp.zeros(carry.shape, jnp.float32)
    for step in reversed(range(1, ctx_size)):
        @pl.when(me >= step)
        def _():
            state_copy(step).wait_recv()
            span = jnp.exp(-float(rows) * rates[...])
            carry[...] = carry[...] * span + state_recv[step - 1].astype(jnp.float32)

    def carried_step(step, state):
        queried = as_tokens(queries[token_rows(step * SUB, SUB), :])
        local = as_tokens(summed[token_rows(step * SUB, SUB), :])
        gated = []
        for within in range(SUB):
            state = decay_step * state
            gated.append((queried[within] * (local[within] + mode_sum(state)))[None])
        summed[token_rows(step * SUB, SUB), :] = as_rows(jnp.concatenate(gated, 0))
        return state

    lax.fori_loop(0, rows // SUB, carried_step, weights * as_tokens(carry[...]))

    padded = squares.shape[0]
    if padded > rows:
        squares[rows:padded, :] = jnp.zeros((padded - rows, LANES), jnp.float32)

    @pl.loop(0, rows // SUB)
    def _(tile):
        first = pl.multiple_of(tile * SUB, SUB)
        total = None
        for group in range(groups):
            part = summed[pl.ds(first * SUB + group, SUB, stride=SUB), :]
            total = part * part if total is None else total + part * part
        squares[pl.ds(first, SUB), :] = total

    own_sum = lax.dot_general(
        jnp.ones((SUB, LANES), jnp.float32),
        squares[...],
        (((1,), (1,)), ((), ())),
        precision=lax.Precision.HIGHEST,
        preferred_element_type=jnp.float32,
    )
    sum_send[...] = own_sum

    def sum_copy(step):
        return pltpu.make_async_remote_copy(
            src_ref=sum_send,
            dst_ref=sum_recv.at[step - 1],
            send_sem=sum_send_sems.at[step - 1],
            recv_sem=sum_recv_sems.at[step - 1],
            device_id={"ch": lax.rem(my_ch + step, ch_size)},
            device_id_type=MESH,
        )

    for step in range(1, ch_size):
        sum_copy(step).start()
    total_sum = own_sum
    for step in range(1, ch_size):
        sum_copy(step).wait_recv()
        total_sum = total_sum + sum_recv[step - 1]
    inverse = lax.rsqrt(total_sum / C + norm_eps)
    same = lax.broadcasted_iota(jnp.int32, (padded, padded), 0) == lax.broadcasted_iota(
        jnp.int32, (padded, padded), 1
    )
    column = jnp.sum(
        jnp.where(same, jnp.broadcast_to(inverse[0:1], (padded, padded)), 0.0), 1, keepdims=True
    )
    squares[...] = jnp.broadcast_to(column, (padded, LANES))

    @pl.loop(0, rows // TILE)
    def _(tile):
        first = pl.multiple_of(tile * TILE, TILE)
        scale = squares[pl.ds(first, TILE), :]
        for group in range(groups):
            part = summed[pl.ds(first * SUB + group, TILE, stride=SUB), :]
            out_ref[pl.ds(first, TILE), lane_group(group)] = (
                part * scale * gain_ref[:, lane_group(group)]
            ).astype(jnp.bfloat16)

    @pl.when(me < ctx_size - 1)
    def _():
        edge_copy.wait_send()
        product_copy.wait_send()

    for step in range(1, ctx_size):
        @pl.when(me + step < ctx_size)
        def _():
            state_copy(step).wait_send()

    for step in range(1, ch_size):
        sum_copy(step).wait_send()


def on_device(
    ctx_size, ch_size, projected, short_filter, medium_filter, decay, residues, skip_gain, out_gain
):
    rows = projected.shape[1]
    chans = projected.shape[2]
    padded = -(-rows // LANES) * LANES
    f32 = jnp.float32
    bf16 = jnp.bfloat16

    def token_buffer(count, dtype=f32):
        return pltpu.VMEM((count * SUB, LANES), dtype)

    dma = pltpu.SemaphoreType.DMA
    vmem = pl.BlockSpec(memory_space=pltpu.VMEM)
    flops = rows * chans * (2 * MED + 6 * SHORT + 8 * MODES)
    return pl.pallas_call(
        functools.partial(block_kernel, ctx_size, ch_size),
        out_shape=jax.ShapeDtypeStruct((rows, chans), bf16),
        in_specs=[pl.BlockSpec(memory_space=pltpu.HBM)] * 7,
        out_specs=vmem,
        scratch_shapes=[
            pltpu.VMEM(projected.shape, bf16),
            pltpu.VMEM((3, SHORT, chans), f32),
            pltpu.VMEM(medium_filter.shape, bf16),
            pltpu.VMEM(decay.shape, f32),
            pltpu.VMEM(residues.shape, f32),
            pltpu.VMEM((chans // LANES, LANES), f32),
            pltpu.VMEM((1, chans), f32),
            dma((9,)),
            token_buffer(LEAD + rows),
            token_buffer(LEAD + rows),
            token_buffer(LEAD + rows),
            token_buffer(SHORT * 3),
            token_buffer(MED),
            pltpu.VMEM((SUBS, (DEPTH + rows // PHASES) * SUB, LANES), f32),
            pltpu.VMEM((SUBS, DEPTH * SUB, LANES), f32),
            pltpu.VMEM((SUBS, (1 + rows // PHASES) * SUB, LANES), f32),
            token_buffer(rows),
            token_buffer(rows),
            token_buffer(rows),
            token_buffer(MODES),
            token_buffer(MODES),
            token_buffer(MODES),
            pltpu.VMEM((padded, LANES), f32),
            pltpu.VMEM((3, TILE, chans), bf16),
            token_buffer(MED, bf16),
            token_buffer(MED, bf16),
            token_buffer(MODES, bf16),
            pltpu.VMEM((ctx_size - 1, MODES * SUB, LANES), bf16),
            pltpu.VMEM((SUB, padded), f32),
            pltpu.VMEM((ch_size - 1, SUB, padded), f32),
            dma((2,)),
            dma((2,)),
            dma((ctx_size - 1,)),
            dma((ctx_size - 1,)),
            dma((ch_size - 1,)),
            dma((ch_size - 1,)),
        ],
        compiler_params=pltpu.CompilerParams(
            collective_id=0, has_side_effects=True, vmem_limit_bytes=63 * 1024 * 1024
        ),
        cost_estimate=pl.CostEstimate(
            flops=flops, bytes_accessed=rows * chans * 8, transcendentals=0
        ),
    )(
        projected,
        jnp.transpose(short_filter, (1, 0, 2)),
        medium_filter,
        decay,
        residues,
        skip_gain.reshape(chans // LANES, LANES),
        out_gain.reshape(1, chans),
    )


def solution(mesh):
    in_specs = (
        P(None, "ctx", "ch"),
        P(None, None, "ch"),
        P(None, "ch"),
        P(None, "ch"),
        P(None, "ch"),
        P("ch"),
        P("ch"),
    )
    out_specs = P("ctx", "ch")
    body = functools.partial(on_device, mesh.shape["ctx"], mesh.shape["ch"])
    return jax.shard_map(
        body, mesh=mesh, in_specs=in_specs, out_specs=out_specs, check_vma=False
    )
```

```python
import functools

import jax
import jax.numpy as jnp
from jax import lax
from jax.experimental import pallas as pl
from jax.experimental.pallas import tpu as pltpu
from jax.sharding import PartitionSpec as P

C = 4096
SHORT = 7
MED = 128
MODES = 16
LANES = 128
SUB = 8
LEAD = 8
TILE = 16
TAPS = 8
PHASES = 4
SUBS = 9
DEPTH = MED // PHASES
norm_eps = 1e-06
MESH = pl.DeviceIdType.MESH


def as_tokens(rows):
    return rows.reshape(rows.shape[0] // SUB, SUB, LANES)


def as_rows(tokens):
    return tokens.reshape(tokens.shape[0] * SUB, LANES)


def token_rows(first, count):
    start = first * SUB
    if not isinstance(start, int):
        start = pl.multiple_of(start, SUB)
    return pl.ds(start, count * SUB)


def phase_parts(tokens):
    quads = tokens.reshape(tokens.shape[0] // PHASES, PHASES, SUB, LANES)
    part00, part10, part01, part11 = (quads[:, phase] for phase in range(PHASES))
    low, high = part00 + part10, part01 + part11
    parts = (
        part00, part01, part00 + part01,
        part10, part11, part10 + part11,
        low, high, low + high,
    )
    return [as_rows(part) for part in parts]


def rounded(tokens):
    return as_tokens(as_rows(tokens).astype(jnp.bfloat16).astype(jnp.float32))


def mode_sum(parts):
    count = parts.shape[0]
    while count > 1:
        count //= 2
        parts = parts[:count] + parts[count:]
    return parts[0]


def block_kernel(
    ctx_size,
    ch_size,
    proj_hbm,
    short_hbm,
    medium_hbm,
    decay_hbm,
    residue_hbm,
    skip_hbm,
    gain_hbm,
    out_ref,
    proj_ref,
    short_ref,
    medium_ref,
    decay_ref,
    residue_ref,
    skip_ref,
    gain_ref,
    load_sems,
    series0,
    series1,
    series2,
    short_taps,
    medium_taps,
    phased,
    phased_taps,
    filtered,
    queries,
    mediated,
    summed,
    rates,
    weights_buf,
    carry,
    squares,
    edge_recv,
    product_send,
    product_recv,
    state_send,
    state_recv,
    sum_send,
    sum_recv,
    edge_sems,
    product_sems,
    state_send_sems,
    state_recv_sems,
    sum_send_sems,
    sum_recv_sems,
):
    rows = proj_ref.shape[1]
    groups = proj_ref.shape[2] // LANES
    series = (series0, series1, series2)
    me = lax.axis_index("ctx")
    my_ch = lax.axis_index("ch")
    following = lax.rem(me + 1, ctx_size)

    pairs = {
        "short": (short_hbm, short_ref),
        "key": (proj_hbm.at[1], proj_ref.at[1]),
        "value": (proj_hbm.at[2], proj_ref.at[2]),
        "medium": (medium_hbm, medium_ref),
        "query": (proj_hbm.at[0], proj_ref.at[0]),
        "decay": (decay_hbm, decay_ref),
        "residue": (residue_hbm, residue_ref),
        "skip": (skip_hbm, skip_ref),
        "gain": (gain_hbm, gain_ref),
    }
    loads = {
        name: pltpu.make_async_copy(source, target, load_sems.at[position])
        for position, (name, (source, target)) in enumerate(pairs.items())
    }
    for load in loads.values():
        load.start()

    barrier = pltpu.get_barrier_semaphore()
    for step in range(1, ctx_size):
        pl.semaphore_signal(
            barrier,
            inc=1,
            device_id={"ctx": lax.rem(me + step, ctx_size)},
            device_id_type=MESH,
        )
    for step in range(1, ch_size):
        pl.semaphore_signal(
            barrier,
            inc=1,
            device_id={"ch": lax.rem(my_ch + step, ch_size)},
            device_id_type=MESH,
        )

    if groups < SUB:
        for ref in (
            series0, series1, series2, short_taps, medium_taps, rates, weights_buf,
        ):
            ref[...] = jnp.zeros(ref.shape, ref.dtype)

    def lane_group(group):
        return slice(group * LANES, (group + 1) * LANES)

    def spread_series(index, low, high):
        @pl.loop(low, high)
        def _(tile):
            first = pl.multiple_of(tile * TILE, TILE)
            for group in range(groups):
                part = proj_ref[index, pl.ds(first, TILE), lane_group(group)]
                series[index][
                    pl.ds((LEAD + first) * SUB + group, TILE, stride=SUB), :
                ] = part.astype(jnp.float32)

    loads["short"].wait()
    for index in range(3):
        for group in range(groups):
            short_taps[pl.ds(index * SHORT * SUB + group, SHORT, stride=SUB), :] = short_ref[
                index, :, lane_group(group)
            ]
    edge_copy = pltpu.make_async_remote_copy(
        src_ref=proj_hbm.at[:, pl.ds(rows - TILE, TILE), :],
        dst_ref=edge_recv,
        send_sem=edge_sems.at[0],
        recv_sem=edge_sems.at[1],
        device_id={"ctx": following},
        device_id_type=MESH,
    )
    half_tiles = MED // (2 * TILE)
    all_tiles = rows // TILE

    def product_copy(half):
        return pltpu.make_async_remote_copy(
            src_ref=product_send.at[half],
            dst_ref=product_recv.at[half],
            send_sem=product_sems.at[0, half],
            recv_sem=product_sems.at[1, half],
            device_id={"ctx": following},
            device_id_type=MESH,
        )

    def featured(index, first):
        window = as_tokens(series[index][token_rows(LEAD + first - (SHORT - 1), TILE + SHORT - 1), :])
        total = None
        for delay in range(SHORT):
            tap = short_taps[(index * SHORT + delay) * SUB : (index * SHORT + delay + 1) * SUB, :]
            offset = SHORT - 1 - delay
            term = tap[None] * window[offset : offset + TILE]
            total = term if total is None else total + term
        return rounded(total)

    def product_tile(first):
        return as_rows(featured(1, first) * featured(2, first)).astype(jnp.bfloat16)

    def keep_product(first, tokens):
        start = pl.multiple_of(first * (SUB // PHASES), TILE * SUB // PHASES)
        for sub, part in enumerate(phase_parts(tokens)):
            phased[sub, pl.ds(start, TILE * SUB // PHASES), :] = part

    def send_half(half):
        low = all_tiles - half_tiles * (half + 1)

        @pl.loop(low, low + half_tiles)
        def _(tile):
            first = tile * TILE
            value = product_tile(first)
            start = pl.multiple_of((tile - low) * (TILE * SUB), TILE * SUB)
            product_send[half, pl.ds(start, TILE * SUB), :] = value
            keep_product(MED + first, as_tokens(value.astype(jnp.float32)))

    def receive_half(half):
        @pl.when(me > 0)
        def _():
            product_copy(half).wait_recv()

            @pl.loop(0, half_tiles)
            def _(tile):
                start = pl.multiple_of(tile * TILE * SUB, TILE * SUB)
                part = product_recv[half, pl.ds(start, TILE * SUB), :].astype(jnp.float32)
                keep_product((tile + half_tiles * (1 - half)) * TILE, as_tokens(part))

    tail = all_tiles - half_tiles - 1
    loads["key"].wait()
    spread_series(1, tail, all_tiles)
    loads["value"].wait()
    spread_series(2, tail, all_tiles)
    send_half(0)
    pl.semaphore_wait(barrier, ctx_size - 1 + ch_size - 1)

    @pl.when(me < ctx_size - 1)
    def _():
        edge_copy.start()
        product_copy(0).start()

    middle = tail - half_tiles
    spread_series(1, middle, tail)
    spread_series(2, middle, tail)
    send_half(1)

    @pl.when(me < ctx_size - 1)
    def _():
        product_copy(1).start()

    spread_series(1, 0, middle)
    spread_series(2, 0, middle)
    loads["medium"].wait()

    @pl.loop(0, MED // TILE)
    def _(tile):
        first = pl.multiple_of(tile * TILE, TILE)
        for group in range(groups):
            part = medium_ref[pl.ds(first, TILE), lane_group(group)]
            medium_taps[pl.ds(first * SUB + group, TILE, stride=SUB), :] = part.astype(jnp.float32)
        start = pl.multiple_of(tile * (TILE * SUB // PHASES), TILE * SUB // PHASES)
        taps = as_tokens(medium_taps[token_rows(first, TILE), :])
        for sub, part in enumerate(phase_parts(taps)):
            phased_taps[sub, pl.ds(start, TILE * SUB // PHASES), :] = part

    loads["query"].wait()
    spread_series(0, 0, all_tiles)

    loads["decay"].wait()
    loads["residue"].wait()
    for group in range(groups):
        rate = decay_ref[:, lane_group(group)]
        twice = 2.0 * rate
        series_form = twice * (
            1.0
            - twice
            * (0.5 - twice * (1.0 / 6.0 - twice * (1.0 / 24.0 - twice * (1.0 / 120.0 - twice / 720.0))))
        )
        power = jnp.where(twice < 0.125, series_form, 1.0 - jnp.exp(-twice))
        rates[pl.ds(group, MODES, stride=SUB), :] = rate
        weights_buf[pl.ds(group, MODES, stride=SUB), :] = residue_ref[
            :, lane_group(group)
        ] * jnp.sqrt(power)

    @pl.when(me > 0)
    def _():
        edge_copy.wait_recv()
        for index in range(3):
            for group in range(groups):
                part = edge_recv[index, :, lane_group(group)].astype(jnp.float32)
                series[index][pl.ds(group, LEAD, stride=SUB), :] = part[TILE - LEAD :]

    @pl.when(me == 0)
    def _():
        for index in range(3):
            series[index][0 : LEAD * SUB, :] = jnp.zeros((LEAD * SUB, LANES), jnp.float32)

    @pl.loop(0, all_tiles - 2 * half_tiles)
    def _(tile):
        first = tile * TILE
        keep_product(MED + first, as_tokens(product_tile(first).astype(jnp.float32)))

    @pl.loop(0, rows // TILE)
    def _(tile):
        first = tile * TILE
        queries[token_rows(first, TILE), :] = as_rows(featured(0, first))

    steps = rows // PHASES

    def sub_filter(sub, first, count):
        total = jnp.zeros((count, SUB, LANES), jnp.float32)
        for delay in range(0, DEPTH, TAPS):
            window = as_tokens(
                phased[sub, token_rows(DEPTH + first - delay - (TAPS - 1), count + TAPS - 1), :]
            )
            taps = as_tokens(phased_taps[sub, token_rows(delay, TAPS), :])
            for within in range(TAPS):
                offset = TAPS - 1 - within
                total = total + taps[within][None] * window[offset : offset + count]
        filtered[sub, token_rows(1 + first, count), :] = as_rows(total)

    def medium_tile(tile):
        @pl.loop(0, SUBS)
        def _(sub):
            sub_filter(sub, tile * TILE, TILE)

    def merge_tile(tile):
        count = TILE // PHASES
        first = tile * count
        wide = [
            as_tokens(filtered[sub, token_rows(first, count + 1), :]) for sub in range(SUBS)
        ]

        def half_rate(base):
            low, high, both = wide[base : base + 3]
            return low[1:] + high[:count], both - low - high

        even0, even1 = half_rate(0)
        odd0, odd1 = half_rate(3)
        both0, both1 = half_rate(6)
        outs = (
            even0 + odd1[:count],
            both0 - even0 - odd0,
            even1[1:] + odd0,
            (both1 - even1 - odd1)[1:],
        )
        tokens = jnp.stack(outs, 1).reshape(TILE, SUB, LANES)
        mediated[token_rows(tile * TILE, TILE), :] = as_rows(rounded(tokens))

    @pl.when(me == 0)
    def _():
        phased[:, 0 : DEPTH * SUB, :] = jnp.zeros((SUBS, DEPTH * SUB, LANES), jnp.float32)

    @pl.loop(DEPTH // TILE, steps // TILE)
    def _(tile):
        medium_tile(tile)

    for half in range(2):
        receive_half(half)
        medium_tile(1 - half)

    @pl.loop(0, SUBS)
    def _(sub):
        sub_filter(sub, -1, 1)

    @pl.loop(0, rows // TILE)
    def _(tile):
        merge_tile(tile)

    decay_step = jnp.exp(-as_tokens(rates[...]))
    weights = as_tokens(weights_buf[...])

    def state_step(step, state):
        inputs = as_tokens(mediated[token_rows(step * SUB, SUB), :])
        for within in range(SUB):
            state = decay_step * state + inputs[within][None]
        return state

    zero_state = jnp.zeros((MODES, SUB, LANES), jnp.float32)
    final = lax.fori_loop(0, rows // SUB, state_step, zero_state)
    state_send[...] = as_rows(final).astype(jnp.bfloat16)

    def state_copy(step):
        return pltpu.make_async_remote_copy(
            src_ref=state_send,
            dst_ref=state_recv.at[step - 1],
            send_sem=state_send_sems.at[step - 1],
            recv_sem=state_recv_sems.at[step - 1],
            device_id={"ctx": lax.rem(me + step, ctx_size)},
            device_id_type=MESH,
        )

    for step in range(1, ctx_size):
        @pl.when(me + step < ctx_size)
        def _():
            state_copy(step).start()

    loads["skip"].wait()
    loads["gain"].wait()
    skip = skip_ref[...]
    if groups < SUB:
        skip = jnp.concatenate([skip, jnp.zeros((SUB - groups, LANES), jnp.float32)], 0)

    def local_step(step, state):
        inputs = as_tokens(mediated[token_rows(step * SUB, SUB), :])
        sums = []
        for within in range(SUB):
            state = decay_step * state + inputs[within][None]
            sums.append((mode_sum(weights * state) + skip * inputs[within])[None])
        summed[token_rows(step * SUB, SUB), :] = as_rows(jnp.concatenate(sums, 0))
        return state

    lax.fori_loop(0, rows // SUB, local_step, zero_state)

    carry[...] = jnp.zeros(carry.shape, jnp.float32)
    for step in reversed(range(1, ctx_size)):
        @pl.when(me >= step)
        def _():
            state_copy(step).wait_recv()
            span = jnp.exp(-float(rows) * rates[...])
            carry[...] = carry[...] * span + state_recv[step - 1].astype(jnp.float32)

    def carried_step(step, state):
        queried = as_tokens(queries[token_rows(step * SUB, SUB), :])
        local = as_tokens(summed[token_rows(step * SUB, SUB), :])
        gated = []
        for within in range(SUB):
            state = decay_step * state
            gated.append((queried[within] * (local[within] + mode_sum(state)))[None])
        summed[token_rows(step * SUB, SUB), :] = as_rows(jnp.concatenate(gated, 0))
        return state

    lax.fori_loop(0, rows // SUB, carried_step, weights * as_tokens(carry[...]))

    padded = squares.shape[0]
    if padded > rows:
        squares[rows:padded, :] = jnp.zeros((padded - rows, LANES), jnp.float32)

    @pl.loop(0, rows // SUB)
    def _(tile):
        first = pl.multiple_of(tile * SUB, SUB)
        total = None
        for group in range(groups):
            part = summed[pl.ds(first * SUB + group, SUB, stride=SUB), :]
            total = part * part if total is None else total + part * part
        squares[pl.ds(first, SUB), :] = total

    own_sum = lax.dot_general(
        jnp.ones((SUB, LANES), jnp.float32),
        squares[...],
        (((1,), (1,)), ((), ())),
        precision=lax.Precision.HIGHEST,
        preferred_element_type=jnp.float32,
    )
    sum_send[...] = own_sum

    def sum_copy(step):
        return pltpu.make_async_remote_copy(
            src_ref=sum_send,
            dst_ref=sum_recv.at[step - 1],
            send_sem=sum_send_sems.at[step - 1],
            recv_sem=sum_recv_sems.at[step - 1],
            device_id={"ch": lax.rem(my_ch + step, ch_size)},
            device_id_type=MESH,
        )

    for step in range(1, ch_size):
        sum_copy(step).start()
    total_sum = own_sum
    for step in range(1, ch_size):
        sum_copy(step).wait_recv()
        total_sum = total_sum + sum_recv[step - 1]
    inverse = lax.rsqrt(total_sum / C + norm_eps)
    same = lax.broadcasted_iota(jnp.int32, (padded, padded), 0) == lax.broadcasted_iota(
        jnp.int32, (padded, padded), 1
    )
    column = jnp.sum(
        jnp.where(same, jnp.broadcast_to(inverse[0:1], (padded, padded)), 0.0), 1, keepdims=True
    )
    squares[...] = jnp.broadcast_to(column, (padded, LANES))

    @pl.loop(0, rows // TILE)
    def _(tile):
        first = pl.multiple_of(tile * TILE, TILE)
        scale = squares[pl.ds(first, TILE), :]
        for group in range(groups):
            part = summed[pl.ds(first * SUB + group, TILE, stride=SUB), :]
            out_ref[pl.ds(first, TILE), lane_group(group)] = (
                part * scale * gain_ref[:, lane_group(group)]
            ).astype(jnp.bfloat16)

    @pl.when(me < ctx_size - 1)
    def _():
        edge_copy.wait_send()
        for half in range(2):
            product_copy(half).wait_send()

    for step in range(1, ctx_size):
        @pl.when(me + step < ctx_size)
        def _():
            state_copy(step).wait_send()

    for step in range(1, ch_size):
        sum_copy(step).wait_send()


def on_device(
    ctx_size, ch_size, projected, short_filter, medium_filter, decay, residues, skip_gain, out_gain
):
    rows = projected.shape[1]
    chans = projected.shape[2]
    padded = -(-rows // LANES) * LANES
    f32 = jnp.float32
    bf16 = jnp.bfloat16

    def token_buffer(count, dtype=f32):
        return pltpu.VMEM((count * SUB, LANES), dtype)

    dma = pltpu.SemaphoreType.DMA
    vmem = pl.BlockSpec(memory_space=pltpu.VMEM)
    flops = rows * chans * (2 * MED + 6 * SHORT + 8 * MODES)
    return pl.pallas_call(
        functools.partial(block_kernel, ctx_size, ch_size),
        out_shape=pltpu.VMEM((rows, chans), bf16),
        in_specs=[pl.BlockSpec(memory_space=pltpu.HBM)] * 7,
        out_specs=vmem,
        scratch_shapes=[
            pltpu.VMEM(projected.shape, bf16),
            pltpu.VMEM((3, SHORT, chans), f32),
            pltpu.VMEM(medium_filter.shape, bf16),
            pltpu.VMEM(decay.shape, f32),
            pltpu.VMEM(residues.shape, f32),
            pltpu.VMEM((chans // LANES, LANES), f32),
            pltpu.VMEM((1, chans), f32),
            dma((9,)),
            token_buffer(LEAD + rows),
            token_buffer(LEAD + rows),
            token_buffer(LEAD + rows),
            token_buffer(SHORT * 3),
            token_buffer(MED),
            pltpu.VMEM((SUBS, (DEPTH + rows // PHASES) * SUB, LANES), f32),
            pltpu.VMEM((SUBS, DEPTH * SUB, LANES), f32),
            pltpu.VMEM((SUBS, (1 + rows // PHASES) * SUB, LANES), f32),
            token_buffer(rows),
            token_buffer(rows),
            token_buffer(rows),
            token_buffer(MODES),
            token_buffer(MODES),
            token_buffer(MODES),
            pltpu.VMEM((padded, LANES), f32),
            pltpu.VMEM((3, TILE, chans), bf16),
            pltpu.VMEM((2, MED * SUB // 2, LANES), bf16),
            pltpu.VMEM((2, MED * SUB // 2, LANES), bf16),
            token_buffer(MODES, bf16),
            pltpu.VMEM((ctx_size - 1, MODES * SUB, LANES), bf16),
            pltpu.VMEM((SUB, padded), f32),
            pltpu.VMEM((ch_size - 1, SUB, padded), f32),
            dma((2,)),
            dma((2, 2)),
            dma((ctx_size - 1,)),
            dma((ctx_size - 1,)),
            dma((ch_size - 1,)),
            dma((ch_size - 1,)),
        ],
        compiler_params=pltpu.CompilerParams(
            collective_id=0, has_side_effects=True, vmem_limit_bytes=40 * 1024 * 1024
        ),
        cost_estimate=pl.CostEstimate(
            flops=flops, bytes_accessed=rows * chans * 8, transcendentals=0
        ),
    )(
        *(
            pltpu.with_memory_space_constraint(operand, pltpu.HBM)
            for operand in (
                projected,
                jnp.transpose(short_filter, (1, 0, 2)),
                medium_filter,
                decay,
                residues,
                skip_gain.reshape(chans // LANES, LANES),
                out_gain.reshape(1, chans),
            )
        )
    )


def solution(mesh):
    in_specs = (
        P(None, "ctx", "ch"),
        P(None, None, "ch"),
        P(None, "ch"),
        P(None, "ch"),
        P(None, "ch"),
        P("ch"),
        P("ch"),
    )
    out_specs = P("ctx", "ch")
    body = functools.partial(on_device, mesh.shape["ctx"], mesh.shape["ch"])
    return jax.shard_map(
        body, mesh=mesh, in_specs=in_specs, out_specs=out_specs, check_vma=False
    )
```

```python
import functools

import jax
import jax.numpy as jnp
from jax import lax
from jax.experimental import pallas as pl
from jax.experimental.pallas import tpu as pltpu
from jax.sharding import PartitionSpec as P

C = 4096
SHORT = 7
MED = 128
MODES = 16
LANES = 128
SUB = 8
LEAD = 8
TILE = 16
TAPS = 8
PHASES = 4
SUBS = 9
DEPTH = MED // PHASES
norm_eps = 1e-06
MESH = pl.DeviceIdType.MESH


def as_tokens(rows):
    return rows.reshape(rows.shape[0] // SUB, SUB, LANES)


def as_rows(tokens):
    return tokens.reshape(tokens.shape[0] * SUB, LANES)


def token_rows(first, count):
    start = first * SUB
    if not isinstance(start, int):
        start = pl.multiple_of(start, SUB)
    return pl.ds(start, count * SUB)


def phase_parts(tokens):
    quads = tokens.reshape(tokens.shape[0] // PHASES, PHASES, SUB, LANES)
    part00, part10, part01, part11 = (quads[:, phase] for phase in range(PHASES))
    low, high = part00 + part10, part01 + part11
    parts = (
        part00, part01, part00 + part01,
        part10, part11, part10 + part11,
        low, high, low + high,
    )
    return [as_rows(part) for part in parts]


def rounded(tokens):
    return as_tokens(as_rows(tokens).astype(jnp.bfloat16).astype(jnp.float32))


def mode_sum(parts):
    count = parts.shape[0]
    while count > 1:
        count //= 2
        parts = parts[:count] + parts[count:]
    return parts[0]


def block_kernel(
    ctx_size,
    ch_size,
    proj_hbm,
    short_hbm,
    medium_hbm,
    decay_hbm,
    residue_hbm,
    skip_hbm,
    gain_hbm,
    out_ref,
    proj_ref,
    short_ref,
    medium_ref,
    decay_ref,
    residue_ref,
    skip_ref,
    gain_ref,
    load_sems,
    series0,
    series1,
    series2,
    short_taps,
    medium_taps,
    phased,
    phased_taps,
    filtered,
    queries,
    mediated,
    summed,
    rates,
    weights_buf,
    carry,
    block_decay,
    head_taps,
    out_table,
    entry_states,
    squares,
    edge_recv,
    product_send,
    product_recv,
    state_send,
    state_recv,
    sum_send,
    sum_recv,
    edge_sems,
    product_sems,
    state_send_sems,
    state_recv_sems,
    sum_send_sems,
    sum_recv_sems,
):
    rows = proj_ref.shape[1]
    groups = proj_ref.shape[2] // LANES
    series = (series0, series1, series2)
    me = lax.axis_index("ctx")
    my_ch = lax.axis_index("ch")
    following = lax.rem(me + 1, ctx_size)

    pairs = {
        "short": (short_hbm, short_ref),
        "key": (proj_hbm.at[1], proj_ref.at[1]),
        "value": (proj_hbm.at[2], proj_ref.at[2]),
        "medium": (medium_hbm, medium_ref),
        "query": (proj_hbm.at[0], proj_ref.at[0]),
        "decay": (decay_hbm, decay_ref),
        "residue": (residue_hbm, residue_ref),
        "skip": (skip_hbm, skip_ref),
        "gain": (gain_hbm, gain_ref),
    }
    loads = {
        name: pltpu.make_async_copy(source, target, load_sems.at[position])
        for position, (name, (source, target)) in enumerate(pairs.items())
    }
    for load in loads.values():
        load.start()

    barrier = pltpu.get_barrier_semaphore()
    for step in range(1, ctx_size):
        pl.semaphore_signal(
            barrier,
            inc=1,
            device_id={"ctx": lax.rem(me + step, ctx_size)},
            device_id_type=MESH,
        )
    for step in range(1, ch_size):
        pl.semaphore_signal(
            barrier,
            inc=1,
            device_id={"ch": lax.rem(my_ch + step, ch_size)},
            device_id_type=MESH,
        )

    if groups < SUB:
        for ref in (
            series0, series1, series2, short_taps, medium_taps, rates, weights_buf,
        ):
            ref[...] = jnp.zeros(ref.shape, ref.dtype)

    def lane_group(group):
        return slice(group * LANES, (group + 1) * LANES)

    def spread_series(index, low, high):
        @pl.loop(low, high)
        def _(tile):
            first = pl.multiple_of(tile * TILE, TILE)
            for group in range(groups):
                part = proj_ref[index, pl.ds(first, TILE), lane_group(group)]
                series[index][
                    pl.ds((LEAD + first) * SUB + group, TILE, stride=SUB), :
                ] = part.astype(jnp.float32)

    loads["short"].wait()
    for index in range(3):
        for group in range(groups):
            short_taps[pl.ds(index * SHORT * SUB + group, SHORT, stride=SUB), :] = short_ref[
                index, :, lane_group(group)
            ]
    edge_copy = pltpu.make_async_remote_copy(
        src_ref=proj_hbm.at[:, pl.ds(rows - TILE, TILE), :],
        dst_ref=edge_recv,
        send_sem=edge_sems.at[0],
        recv_sem=edge_sems.at[1],
        device_id={"ctx": following},
        device_id_type=MESH,
    )
    half_tiles = MED // (2 * TILE)
    all_tiles = rows // TILE

    def product_copy(half):
        return pltpu.make_async_remote_copy(
            src_ref=product_send.at[half],
            dst_ref=product_recv.at[half],
            send_sem=product_sems.at[0, half],
            recv_sem=product_sems.at[1, half],
            device_id={"ctx": following},
            device_id_type=MESH,
        )

    def featured(index, first):
        window = as_tokens(series[index][token_rows(LEAD + first - (SHORT - 1), TILE + SHORT - 1), :])
        total = None
        for delay in range(SHORT):
            tap = short_taps[(index * SHORT + delay) * SUB : (index * SHORT + delay + 1) * SUB, :]
            offset = SHORT - 1 - delay
            term = tap[None] * window[offset : offset + TILE]
            total = term if total is None else total + term
        return rounded(total)

    def product_tile(first):
        return as_rows(featured(1, first) * featured(2, first)).astype(jnp.bfloat16)

    def keep_product(first, tokens):
        start = pl.multiple_of(first * (SUB // PHASES), TILE * SUB // PHASES)
        for sub, part in enumerate(phase_parts(tokens)):
            phased[sub, pl.ds(start, TILE * SUB // PHASES), :] = part

    def send_half(half):
        low = all_tiles - half_tiles * (half + 1)

        @pl.loop(low, low + half_tiles)
        def _(tile):
            first = tile * TILE
            value = product_tile(first)
            start = pl.multiple_of((tile - low) * (TILE * SUB), TILE * SUB)
            product_send[half, pl.ds(start, TILE * SUB), :] = value
            keep_product(MED + first, as_tokens(value.astype(jnp.float32)))

    def receive_half(half):
        @pl.when(me > 0)
        def _():
            product_copy(half).wait_recv()

            @pl.loop(0, half_tiles)
            def _(tile):
                start = pl.multiple_of(tile * TILE * SUB, TILE * SUB)
                part = product_recv[half, pl.ds(start, TILE * SUB), :].astype(jnp.float32)
                keep_product((tile + half_tiles * (1 - half)) * TILE, as_tokens(part))

    tail = all_tiles - half_tiles - 1
    loads["key"].wait()
    spread_series(1, tail, all_tiles)
    loads["value"].wait()
    spread_series(2, tail, all_tiles)
    send_half(0)
    pl.semaphore_wait(barrier, ctx_size - 1 + ch_size - 1)

    @pl.when(me < ctx_size - 1)
    def _():
        edge_copy.start()
        product_copy(0).start()

    middle = tail - half_tiles
    spread_series(1, middle, tail)
    spread_series(2, middle, tail)
    send_half(1)

    @pl.when(me < ctx_size - 1)
    def _():
        product_copy(1).start()

    spread_series(1, 0, middle)
    spread_series(2, 0, middle)
    loads["medium"].wait()

    @pl.loop(0, MED // TILE)
    def _(tile):
        first = pl.multiple_of(tile * TILE, TILE)
        for group in range(groups):
            part = medium_ref[pl.ds(first, TILE), lane_group(group)]
            medium_taps[pl.ds(first * SUB + group, TILE, stride=SUB), :] = part.astype(jnp.float32)
        start = pl.multiple_of(tile * (TILE * SUB // PHASES), TILE * SUB // PHASES)
        taps = as_tokens(medium_taps[token_rows(first, TILE), :])
        for sub, part in enumerate(phase_parts(taps)):
            phased_taps[sub, pl.ds(start, TILE * SUB // PHASES), :] = part

    loads["decay"].wait()
    loads["residue"].wait()
    for group in range(groups):
        rate = decay_ref[:, lane_group(group)]
        twice = 2.0 * rate
        series_form = twice * (
            1.0
            - twice
            * (0.5 - twice * (1.0 / 6.0 - twice * (1.0 / 24.0 - twice * (1.0 / 120.0 - twice / 720.0))))
        )
        power = jnp.where(twice < 0.125, series_form, 1.0 - jnp.exp(-twice))
        rates[pl.ds(group, MODES, stride=SUB), :] = rate
        weights_buf[pl.ds(group, MODES, stride=SUB), :] = residue_ref[
            :, lane_group(group)
        ] * jnp.sqrt(power)

    loads["skip"].wait()
    loads["gain"].wait()
    skip = skip_ref[...]
    if groups < SUB:
        skip = jnp.concatenate([skip, jnp.zeros((SUB - groups, LANES), jnp.float32)], 0)

    decay_step = jnp.exp(-as_tokens(rates[...]))
    weights = as_tokens(weights_buf[...])
    block_decay[...] = jnp.exp(-float(TILE) * rates[...])
    head_taps[0:SUB, :] = mode_sum(weights) + skip

    def table_step(step, table):
        table = decay_step * table
        out_table[step] = as_rows(table)
        head_taps[token_rows(step + 1, 1), :] = mode_sum(table)
        return table

    lax.fori_loop(0, TILE, table_step, weights)

    @pl.when(me > 0)
    def _():
        edge_copy.wait_recv()
        for index in range(3):
            for group in range(groups):
                part = edge_recv[index, :, lane_group(group)].astype(jnp.float32)
                series[index][pl.ds(group, LEAD, stride=SUB), :] = part[TILE - LEAD :]

    @pl.when(me == 0)
    def _():
        for index in range(3):
            series[index][0 : LEAD * SUB, :] = jnp.zeros((LEAD * SUB, LANES), jnp.float32)

    @pl.loop(0, all_tiles - 2 * half_tiles)
    def _(tile):
        first = tile * TILE
        keep_product(MED + first, as_tokens(product_tile(first).astype(jnp.float32)))

    steps = rows // PHASES

    def sub_filter(sub, first, count):
        total = jnp.zeros((count, SUB, LANES), jnp.float32)
        for delay in range(0, DEPTH, TAPS):
            window = as_tokens(
                phased[sub, token_rows(DEPTH + first - delay - (TAPS - 1), count + TAPS - 1), :]
            )
            taps = as_tokens(phased_taps[sub, token_rows(delay, TAPS), :])
            for within in range(TAPS):
                offset = TAPS - 1 - within
                total = total + taps[within][None] * window[offset : offset + count]
        filtered[sub, token_rows(1 + first, count), :] = as_rows(total)

    def medium_tile(tile):
        @pl.loop(0, SUBS)
        def _(sub):
            sub_filter(sub, tile * TILE, TILE)

    def merge_tile(tile):
        count = TILE // PHASES
        first = tile * count
        wide = [
            as_tokens(filtered[sub, token_rows(first, count + 1), :]) for sub in range(SUBS)
        ]

        def half_rate(base):
            low, high, both = wide[base : base + 3]
            return low[1:] + high[:count], both - low - high

        even0, even1 = half_rate(0)
        odd0, odd1 = half_rate(3)
        both0, both1 = half_rate(6)
        outs = (
            even0 + odd1[:count],
            both0 - even0 - odd0,
            even1[1:] + odd0,
            (both1 - even1 - odd1)[1:],
        )
        tokens = jnp.stack(outs, 1).reshape(TILE, SUB, LANES)
        mediated[token_rows(tile * TILE, TILE), :] = as_rows(rounded(tokens))

    @pl.when(me == 0)
    def _():
        phased[:, 0 : DEPTH * SUB, :] = jnp.zeros((SUBS, DEPTH * SUB, LANES), jnp.float32)

    @pl.loop(DEPTH // TILE, steps // TILE)
    def _(tile):
        medium_tile(tile)

    for half in range(2):
        receive_half(half)
        medium_tile(1 - half)

    @pl.loop(0, SUBS)
    def _(sub):
        sub_filter(sub, -1, 1)

    @pl.loop(0, rows // TILE)
    def _(tile):
        merge_tile(tile)

    zero_state = jnp.zeros((MODES, SUB, LANES), jnp.float32)

    def state_step(block, state):
        entry_states[block] = as_rows(state)
        inputs = as_tokens(mediated[token_rows(block * TILE, TILE), :])
        step_decay = jnp.exp(-as_tokens(rates[...]))
        for within in range(TILE):
            state = step_decay * state + inputs[within][None]
        return state

    final = lax.fori_loop(0, all_tiles, state_step, zero_state)
    state_send[...] = as_rows(final).astype(jnp.bfloat16)

    def state_copy(step):
        return pltpu.make_async_remote_copy(
            src_ref=state_send,
            dst_ref=state_recv.at[step - 1],
            send_sem=state_send_sems.at[step - 1],
            recv_sem=state_recv_sems.at[step - 1],
            device_id={"ctx": lax.rem(me + step, ctx_size)},
            device_id_type=MESH,
        )

    for step in range(1, ctx_size):
        @pl.when(me + step < ctx_size)
        def _():
            state_copy(step).start()

    loads["query"].wait()
    spread_series(0, 0, all_tiles)

    @pl.loop(0, rows // TILE)
    def _(tile):
        first = tile * TILE
        queries[token_rows(first, TILE), :] = as_rows(featured(0, first))

    @pl.loop(0, all_tiles)
    def _(block):
        inputs = as_tokens(mediated[token_rows(block * TILE, TILE), :])
        taps = as_tokens(head_taps[0 : TILE * SUB, :])
        sums = [taps[0] * inputs[step] for step in range(TILE)]
        for delay in range(1, TILE):
            for step in range(delay, TILE):
                sums[step] = sums[step] + taps[delay] * inputs[step - delay]
        summed[token_rows(block * TILE, TILE), :] = as_rows(jnp.stack(sums, 0))

    carry[...] = jnp.zeros(carry.shape, jnp.float32)
    for step in reversed(range(1, ctx_size)):
        @pl.when(me >= step)
        def _():
            state_copy(step).wait_recv()
            span = jnp.exp(-float(rows) * rates[...])
            carry[...] = carry[...] * span + state_recv[step - 1].astype(jnp.float32)

    @pl.loop(0, all_tiles // 2)
    def _(pair):
        states = []
        for member in range(2):
            arrived = carry[...]
            states.append(as_tokens(entry_states[pair * 2 + member] + arrived))
            carry[...] = arrived * block_decay[...]
        sums = ([], [])
        for step in range(TILE):
            table = as_tokens(out_table[step])
            for member in range(2):
                sums[member].append(mode_sum(table * states[member]))
        for member in range(2):
            here = token_rows((pair * 2 + member) * TILE, TILE)
            total = as_rows(jnp.stack(sums[member], 0)) + summed[here, :]
            summed[here, :] = queries[here, :] * total

    padded = squares.shape[0]
    if padded > rows:
        squares[rows:padded, :] = jnp.zeros((padded - rows, LANES), jnp.float32)

    @pl.loop(0, rows // SUB)
    def _(tile):
        first = pl.multiple_of(tile * SUB, SUB)
        total = None
        for group in range(groups):
            part = summed[pl.ds(first * SUB + group, SUB, stride=SUB), :]
            total = part * part if total is None else total + part * part
        squares[pl.ds(first, SUB), :] = total

    own_sum = lax.dot_general(
        jnp.ones((SUB, LANES), jnp.float32),
        squares[...],
        (((1,), (1,)), ((), ())),
        precision=lax.Precision.HIGHEST,
        preferred_element_type=jnp.float32,
    )
    sum_send[...] = own_sum

    def sum_copy(step):
        return pltpu.make_async_remote_copy(
            src_ref=sum_send,
            dst_ref=sum_recv.at[step - 1],
            send_sem=sum_send_sems.at[step - 1],
            recv_sem=sum_recv_sems.at[step - 1],
            device_id={"ch": lax.rem(my_ch + step, ch_size)},
            device_id_type=MESH,
        )

    for step in range(1, ch_size):
        sum_copy(step).start()
    total_sum = own_sum
    for step in range(1, ch_size):
        sum_copy(step).wait_recv()
        total_sum = total_sum + sum_recv[step - 1]
    inverse = lax.rsqrt(total_sum / C + norm_eps)
    same = lax.broadcasted_iota(jnp.int32, (padded, padded), 0) == lax.broadcasted_iota(
        jnp.int32, (padded, padded), 1
    )
    column = jnp.sum(
        jnp.where(same, jnp.broadcast_to(inverse[0:1], (padded, padded)), 0.0), 1, keepdims=True
    )
    squares[...] = jnp.broadcast_to(column, (padded, LANES))

    @pl.loop(0, rows // TILE)
    def _(tile):
        first = pl.multiple_of(tile * TILE, TILE)
        scale = squares[pl.ds(first, TILE), :]
        for group in range(groups):
            part = summed[pl.ds(first * SUB + group, TILE, stride=SUB), :]
            out_ref[pl.ds(first, TILE), lane_group(group)] = (
                part * scale * gain_ref[:, lane_group(group)]
            ).astype(jnp.bfloat16)

    @pl.when(me < ctx_size - 1)
    def _():
        edge_copy.wait_send()
        for half in range(2):
            product_copy(half).wait_send()

    for step in range(1, ctx_size):
        @pl.when(me + step < ctx_size)
        def _():
            state_copy(step).wait_send()

    for step in range(1, ch_size):
        sum_copy(step).wait_send()


def on_device(
    ctx_size, ch_size, projected, short_filter, medium_filter, decay, residues, skip_gain, out_gain
):
    rows = projected.shape[1]
    chans = projected.shape[2]
    padded = -(-rows // LANES) * LANES
    f32 = jnp.float32
    bf16 = jnp.bfloat16

    def token_buffer(count, dtype=f32):
        return pltpu.VMEM((count * SUB, LANES), dtype)

    dma = pltpu.SemaphoreType.DMA
    vmem = pl.BlockSpec(memory_space=pltpu.VMEM)
    flops = rows * chans * (2 * MED + 6 * SHORT + 8 * MODES)
    return pl.pallas_call(
        functools.partial(block_kernel, ctx_size, ch_size),
        out_shape=pltpu.VMEM((rows, chans), bf16),
        in_specs=[pl.BlockSpec(memory_space=pltpu.HBM)] * 7,
        out_specs=vmem,
        scratch_shapes=[
            pltpu.VMEM(projected.shape, bf16),
            pltpu.VMEM((3, SHORT, chans), f32),
            pltpu.VMEM(medium_filter.shape, bf16),
            pltpu.VMEM(decay.shape, f32),
            pltpu.VMEM(residues.shape, f32),
            pltpu.VMEM((chans // LANES, LANES), f32),
            pltpu.VMEM((1, chans), f32),
            dma((9,)),
            token_buffer(LEAD + rows),
            token_buffer(LEAD + rows),
            token_buffer(LEAD + rows),
            token_buffer(SHORT * 3),
            token_buffer(MED),
            pltpu.VMEM((SUBS, (DEPTH + rows // PHASES) * SUB, LANES), f32),
            pltpu.VMEM((SUBS, DEPTH * SUB, LANES), f32),
            pltpu.VMEM((SUBS, (1 + rows // PHASES) * SUB, LANES), f32),
            token_buffer(rows),
            token_buffer(rows),
            token_buffer(rows),
            token_buffer(MODES),
            token_buffer(MODES),
            token_buffer(MODES),
            token_buffer(MODES),
            token_buffer(TILE + 1),
            pltpu.VMEM((TILE, MODES * SUB, LANES), f32),
            pltpu.VMEM((rows // TILE, MODES * SUB, LANES), f32),
            pltpu.VMEM((padded, LANES), f32),
            pltpu.VMEM((3, TILE, chans), bf16),
            pltpu.VMEM((2, MED * SUB // 2, LANES), bf16),
            pltpu.VMEM((2, MED * SUB // 2, LANES), bf16),
            token_buffer(MODES, bf16),
            pltpu.VMEM((ctx_size - 1, MODES * SUB, LANES), bf16),
            pltpu.VMEM((SUB, padded), f32),
            pltpu.VMEM((ch_size - 1, SUB, padded), f32),
            dma((2,)),
            dma((2, 2)),
            dma((ctx_size - 1,)),
            dma((ctx_size - 1,)),
            dma((ch_size - 1,)),
            dma((ch_size - 1,)),
        ],
        compiler_params=pltpu.CompilerParams(
            collective_id=0, has_side_effects=True, vmem_limit_bytes=40 * 1024 * 1024
        ),
        cost_estimate=pl.CostEstimate(
            flops=flops, bytes_accessed=rows * chans * 8, transcendentals=0
        ),
    )(
        *(
            pltpu.with_memory_space_constraint(operand, pltpu.HBM)
            for operand in (
                projected,
                jnp.transpose(short_filter, (1, 0, 2)),
                medium_filter,
                decay,
                residues,
                skip_gain.reshape(chans // LANES, LANES),
                out_gain.reshape(1, chans),
            )
        )
    )


def solution(mesh):
    in_specs = (
        P(None, "ctx", "ch"),
        P(None, None, "ch"),
        P(None, "ch"),
        P(None, "ch"),
        P(None, "ch"),
        P("ch"),
        P("ch"),
    )
    out_specs = P("ctx", "ch")
    body = functools.partial(on_device, mesh.shape["ctx"], mesh.shape["ch"])
    return jax.shard_map(
        body, mesh=mesh, in_specs=in_specs, out_specs=out_specs, check_vma=False
    )
```

```python
import functools

import jax
import jax.numpy as jnp
from jax import lax
from jax.experimental import pallas as pl
from jax.experimental.pallas import tpu as pltpu
from jax.sharding import PartitionSpec as P

C = 4096
SHORT = 7
MED = 128
MODES = 16
LANES = 128
SUB = 8
LEAD = 8
TILE = 16
TAPS = 8
PHASES = 4
SUBS = 9
DEPTH = MED // PHASES
norm_eps = 1e-06
MESH = pl.DeviceIdType.MESH


def as_tokens(rows):
    return rows.reshape(rows.shape[0] // SUB, SUB, LANES)


def as_rows(tokens):
    return tokens.reshape(tokens.shape[0] * SUB, LANES)


def token_rows(first, count):
    start = first * SUB
    if not isinstance(start, int):
        start = pl.multiple_of(start, SUB)
    return pl.ds(start, count * SUB)


def phase_parts(tokens):
    quads = tokens.reshape(tokens.shape[0] // PHASES, PHASES, SUB, LANES)
    part00, part10, part01, part11 = (quads[:, phase] for phase in range(PHASES))
    low, high = part00 + part10, part01 + part11
    parts = (
        part00, part01, part00 + part01,
        part10, part11, part10 + part11,
        low, high, low + high,
    )
    return [as_rows(part) for part in parts]


def gather_groups(parts):
    blank = jnp.zeros(parts[0].shape, jnp.float32)
    parts = list(parts) + [blank] * (SUB - len(parts))
    return jnp.transpose(jnp.stack(parts, 0), (1, 0, 2))


def rounded(tokens):
    return as_tokens(as_rows(tokens).astype(jnp.bfloat16).astype(jnp.float32))


def mode_sum(parts):
    count = parts.shape[0]
    while count > 1:
        count //= 2
        parts = parts[:count] + parts[count:]
    return parts[0]


def block_kernel(
    ctx_size,
    ch_size,
    proj_hbm,
    short_hbm,
    medium_hbm,
    decay_hbm,
    residue_hbm,
    skip_hbm,
    gain_hbm,
    out_ref,
    proj_ref,
    short_ref,
    medium_ref,
    decay_ref,
    residue_ref,
    skip_ref,
    gain_ref,
    load_sems,
    series0,
    series1,
    series2,
    short_taps,
    phased,
    phased_taps,
    filtered,
    queries,
    mediated,
    summed,
    rates,
    weights_buf,
    carry,
    block_decay,
    head_taps,
    out_table,
    entry_states,
    flat,
    squares,
    edge_recv,
    product_send,
    product_recv,
    state_send,
    state_recv,
    sum_send,
    sum_recv,
    edge_sems,
    product_sems,
    state_send_sems,
    state_recv_sems,
    sum_send_sems,
    sum_recv_sems,
):
    rows = proj_ref.shape[1]
    groups = proj_ref.shape[2] // LANES
    series = (series0, series1, series2)
    me = lax.axis_index("ctx")
    my_ch = lax.axis_index("ch")
    following = lax.rem(me + 1, ctx_size)

    pairs = {
        "short": (short_hbm, short_ref),
        "key": (proj_hbm.at[1], proj_ref.at[1]),
        "value": (proj_hbm.at[2], proj_ref.at[2]),
        "medium": (medium_hbm, medium_ref),
        "query": (proj_hbm.at[0], proj_ref.at[0]),
        "decay": (decay_hbm, decay_ref),
        "residue": (residue_hbm, residue_ref),
        "skip": (skip_hbm, skip_ref),
        "gain": (gain_hbm, gain_ref),
    }
    loads = {
        name: pltpu.make_async_copy(source, target, load_sems.at[position])
        for position, (name, (source, target)) in enumerate(pairs.items())
    }
    for load in loads.values():
        load.start()

    barrier = pltpu.get_barrier_semaphore()
    for step in range(1, ctx_size):
        pl.semaphore_signal(
            barrier,
            inc=1,
            device_id={"ctx": lax.rem(me + step, ctx_size)},
            device_id_type=MESH,
        )
    for step in range(1, ch_size):
        pl.semaphore_signal(
            barrier,
            inc=1,
            device_id={"ch": lax.rem(my_ch + step, ch_size)},
            device_id_type=MESH,
        )

    if groups < SUB:
        for ref in (
            series0, series1, series2, short_taps, rates, weights_buf,
        ):
            ref[...] = jnp.zeros(ref.shape, ref.dtype)

    def lane_group(group):
        return slice(group * LANES, (group + 1) * LANES)

    def spread_series(index, low, high):
        @pl.loop(low, high)
        def _(tile):
            first = pl.multiple_of(tile * TILE, TILE)
            tokens = gather_groups(
                [
                    proj_ref[index, pl.ds(first, TILE), lane_group(group)].astype(jnp.float32)
                    for group in range(groups)
                ]
            )
            series[index][token_rows(LEAD + first, TILE), :] = as_rows(tokens)

    loads["short"].wait()
    for index in range(3):
        for group in range(groups):
            short_taps[pl.ds(index * SHORT * SUB + group, SHORT, stride=SUB), :] = short_ref[
                index, :, lane_group(group)
            ]
    edge_copy = pltpu.make_async_remote_copy(
        src_ref=proj_hbm.at[:, pl.ds(rows - TILE, TILE), :],
        dst_ref=edge_recv,
        send_sem=edge_sems.at[0],
        recv_sem=edge_sems.at[1],
        device_id={"ctx": following},
        device_id_type=MESH,
    )
    half_tiles = MED // (2 * TILE)
    all_tiles = rows // TILE

    def product_copy(half):
        return pltpu.make_async_remote_copy(
            src_ref=product_send.at[half],
            dst_ref=product_recv.at[half],
            send_sem=product_sems.at[0, half],
            recv_sem=product_sems.at[1, half],
            device_id={"ctx": following},
            device_id_type=MESH,
        )

    def featured(index, first):
        window = as_tokens(series[index][token_rows(LEAD + first - (SHORT - 1), TILE + SHORT - 1), :])
        total = None
        for delay in range(SHORT):
            tap = short_taps[(index * SHORT + delay) * SUB : (index * SHORT + delay + 1) * SUB, :]
            offset = SHORT - 1 - delay
            term = tap[None] * window[offset : offset + TILE]
            total = term if total is None else total + term
        return rounded(total)

    def product_tile(first):
        return as_rows(featured(1, first) * featured(2, first)).astype(jnp.bfloat16)

    def keep_product(first, tokens):
        start = pl.multiple_of(first * (SUB // PHASES), TILE * SUB // PHASES)
        for sub, part in enumerate(phase_parts(tokens)):
            phased[sub, pl.ds(start, TILE * SUB // PHASES), :] = part

    def send_half(half):
        low = all_tiles - half_tiles * (half + 1)

        @pl.loop(low, low + half_tiles)
        def _(tile):
            first = tile * TILE
            value = product_tile(first)
            start = pl.multiple_of((tile - low) * (TILE * SUB), TILE * SUB)
            product_send[half, pl.ds(start, TILE * SUB), :] = value
            keep_product(MED + first, as_tokens(value.astype(jnp.float32)))

    def receive_half(half):
        @pl.when(me > 0)
        def _():
            product_copy(half).wait_recv()

            @pl.loop(0, half_tiles)
            def _(tile):
                start = pl.multiple_of(tile * TILE * SUB, TILE * SUB)
                part = product_recv[half, pl.ds(start, TILE * SUB), :].astype(jnp.float32)
                keep_product((tile + half_tiles * (1 - half)) * TILE, as_tokens(part))

    tail = all_tiles - half_tiles - 1
    loads["key"].wait()
    spread_series(1, tail, all_tiles)
    loads["value"].wait()
    spread_series(2, tail, all_tiles)
    send_half(0)
    pl.semaphore_wait(barrier, ctx_size - 1 + ch_size - 1)

    @pl.when(me < ctx_size - 1)
    def _():
        edge_copy.start()
        product_copy(0).start()

    middle = tail - half_tiles
    spread_series(1, middle, tail)
    spread_series(2, middle, tail)
    send_half(1)

    @pl.when(me < ctx_size - 1)
    def _():
        product_copy(1).start()

    spread_series(1, 0, middle)
    spread_series(2, 0, middle)
    loads["medium"].wait()

    @pl.loop(0, MED // TILE)
    def _(tile):
        first = pl.multiple_of(tile * TILE, TILE)
        taps = gather_groups(
            [
                medium_ref[pl.ds(first, TILE), lane_group(group)].astype(jnp.float32)
                for group in range(groups)
            ]
        )
        start = pl.multiple_of(tile * (TILE * SUB // PHASES), TILE * SUB // PHASES)
        for sub, part in enumerate(phase_parts(taps)):
            phased_taps[sub, pl.ds(start, TILE * SUB // PHASES), :] = part

    loads["decay"].wait()
    loads["residue"].wait()
    for group in range(groups):
        rate = decay_ref[:, lane_group(group)]
        twice = 2.0 * rate
        series_form = twice * (
            1.0
            - twice
            * (0.5 - twice * (1.0 / 6.0 - twice * (1.0 / 24.0 - twice * (1.0 / 120.0 - twice / 720.0))))
        )
        power = jnp.where(twice < 0.125, series_form, 1.0 - jnp.exp(-twice))
        rates[pl.ds(group, MODES, stride=SUB), :] = rate
        weights_buf[pl.ds(group, MODES, stride=SUB), :] = residue_ref[
            :, lane_group(group)
        ] * jnp.sqrt(power)

    loads["skip"].wait()
    loads["gain"].wait()
    skip = skip_ref[...]
    if groups < SUB:
        skip = jnp.concatenate([skip, jnp.zeros((SUB - groups, LANES), jnp.float32)], 0)

    decay_step = jnp.exp(-as_tokens(rates[...]))
    weights = as_tokens(weights_buf[...])
    block_decay[...] = jnp.exp(-float(TILE) * rates[...])
    head_taps[0:SUB, :] = mode_sum(weights) + skip

    def table_step(step, table):
        table = decay_step * table
        out_table[step] = as_rows(table)
        head_taps[token_rows(step + 1, 1), :] = mode_sum(table)
        return table

    lax.fori_loop(0, TILE, table_step, weights)

    @pl.when(me > 0)
    def _():
        edge_copy.wait_recv()
        for index in range(3):
            for group in range(groups):
                part = edge_recv[index, :, lane_group(group)].astype(jnp.float32)
                series[index][pl.ds(group, LEAD, stride=SUB), :] = part[TILE - LEAD :]

    @pl.when(me == 0)
    def _():
        for index in range(3):
            series[index][0 : LEAD * SUB, :] = jnp.zeros((LEAD * SUB, LANES), jnp.float32)

    @pl.loop(0, all_tiles - 2 * half_tiles)
    def _(tile):
        first = tile * TILE
        keep_product(MED + first, as_tokens(product_tile(first).astype(jnp.float32)))

    steps = rows // PHASES

    def sub_filter(sub, first, count):
        total = jnp.zeros((count, SUB, LANES), jnp.float32)
        for delay in range(0, DEPTH, TAPS):
            window = as_tokens(
                phased[sub, token_rows(DEPTH + first - delay - (TAPS - 1), count + TAPS - 1), :]
            )
            taps = as_tokens(phased_taps[sub, token_rows(delay, TAPS), :])
            for within in range(TAPS):
                offset = TAPS - 1 - within
                total = total + taps[within][None] * window[offset : offset + count]
        filtered[sub, token_rows(1 + first, count), :] = as_rows(total)

    def medium_tile(tile):
        @pl.loop(0, SUBS)
        def _(sub):
            sub_filter(sub, tile * TILE, TILE)

    def merge_tile(tile):
        count = TILE // PHASES
        first = tile * count
        wide = [
            as_tokens(filtered[sub, token_rows(first, count + 1), :]) for sub in range(SUBS)
        ]

        def half_rate(base):
            low, high, both = wide[base : base + 3]
            return low[1:] + high[:count], both - low - high

        even0, even1 = half_rate(0)
        odd0, odd1 = half_rate(3)
        both0, both1 = half_rate(6)
        outs = (
            even0 + odd1[:count],
            both0 - even0 - odd0,
            even1[1:] + odd0,
            (both1 - even1 - odd1)[1:],
        )
        tokens = jnp.stack(outs, 1).reshape(TILE, SUB, LANES)
        mediated[token_rows(tile * TILE, TILE), :] = as_rows(rounded(tokens))

    @pl.when(me == 0)
    def _():
        phased[:, 0 : DEPTH * SUB, :] = jnp.zeros((SUBS, DEPTH * SUB, LANES), jnp.float32)

    @pl.loop(DEPTH // TILE, steps // TILE)
    def _(tile):
        medium_tile(tile)

    for half in range(2):
        receive_half(half)
        medium_tile(1 - half)

    @pl.loop(0, SUBS)
    def _(sub):
        sub_filter(sub, -1, 1)

    @pl.loop(0, rows // TILE)
    def _(tile):
        merge_tile(tile)

    zero_state = jnp.zeros((MODES, SUB, LANES), jnp.float32)

    def state_step(block, state):
        entry_states[block] = as_rows(state)
        inputs = as_tokens(mediated[token_rows(block * TILE, TILE), :])
        step_decay = jnp.exp(-as_tokens(rates[...]))
        for within in range(TILE):
            state = step_decay * state + inputs[within][None]
        return state

    final = lax.fori_loop(0, all_tiles, state_step, zero_state)
    state_send[...] = as_rows(final).astype(jnp.bfloat16)

    def state_copy(step):
        return pltpu.make_async_remote_copy(
            src_ref=state_send,
            dst_ref=state_recv.at[step - 1],
            send_sem=state_send_sems.at[step - 1],
            recv_sem=state_recv_sems.at[step - 1],
            device_id={"ctx": lax.rem(me + step, ctx_size)},
            device_id_type=MESH,
        )

    for step in range(1, ctx_size):
        @pl.when(me + step < ctx_size)
        def _():
            state_copy(step).start()

    loads["query"].wait()
    spread_series(0, 0, all_tiles)

    @pl.loop(0, rows // TILE)
    def _(tile):
        first = tile * TILE
        queries[token_rows(first, TILE), :] = as_rows(featured(0, first))

    @pl.loop(0, all_tiles)
    def _(block):
        inputs = as_tokens(mediated[token_rows(block * TILE, TILE), :])
        taps = as_tokens(head_taps[0 : TILE * SUB, :])
        sums = [taps[0] * inputs[step] for step in range(TILE)]
        for delay in range(1, TILE):
            for step in range(delay, TILE):
                sums[step] = sums[step] + taps[delay] * inputs[step - delay]
        summed[token_rows(block * TILE, TILE), :] = as_rows(jnp.stack(sums, 0))

    carry[...] = jnp.zeros(carry.shape, jnp.float32)
    for step in reversed(range(1, ctx_size)):
        @pl.when(me >= step)
        def _():
            state_copy(step).wait_recv()
            span = jnp.exp(-float(rows) * rates[...])
            carry[...] = carry[...] * span + state_recv[step - 1].astype(jnp.float32)

    @pl.loop(0, all_tiles // 2)
    def _(pair):
        states = []
        for member in range(2):
            arrived = carry[...]
            states.append(as_tokens(entry_states[pair * 2 + member] + arrived))
            carry[...] = arrived * block_decay[...]
        sums = ([], [])
        for step in range(TILE):
            table = as_tokens(out_table[step])
            for member in range(2):
                sums[member].append(mode_sum(table * states[member]))
        for member in range(2):
            here = token_rows((pair * 2 + member) * TILE, TILE)
            total = as_rows(jnp.stack(sums[member], 0)) + summed[here, :]
            summed[here, :] = queries[here, :] * total

    padded = squares.shape[0]
    if padded > rows:
        squares[rows:padded, :] = jnp.zeros((padded - rows, LANES), jnp.float32)

    @pl.loop(0, all_tiles)
    def _(tile):
        first = pl.multiple_of(tile * TILE, TILE)
        parts = jnp.transpose(as_tokens(summed[token_rows(first, TILE), :]), (1, 0, 2))
        total = None
        for group in range(groups):
            part = parts[group]
            total = part * part if total is None else total + part * part
            flat[pl.ds(first, TILE), lane_group(group)] = part
        squares[pl.ds(first, TILE), :] = total

    own_sum = lax.dot_general(
        jnp.ones((SUB, LANES), jnp.float32),
        squares[...],
        (((1,), (1,)), ((), ())),
        precision=lax.Precision.HIGHEST,
        preferred_element_type=jnp.float32,
    )
    sum_send[...] = own_sum

    def sum_copy(step):
        return pltpu.make_async_remote_copy(
            src_ref=sum_send,
            dst_ref=sum_recv.at[step - 1],
            send_sem=sum_send_sems.at[step - 1],
            recv_sem=sum_recv_sems.at[step - 1],
            device_id={"ch": lax.rem(my_ch + step, ch_size)},
            device_id_type=MESH,
        )

    for step in range(1, ch_size):
        sum_copy(step).start()
    total_sum = own_sum
    for step in range(1, ch_size):
        sum_copy(step).wait_recv()
        total_sum = total_sum + sum_recv[step - 1]
    inverse = lax.rsqrt(total_sum / C + norm_eps)
    same = lax.broadcasted_iota(jnp.int32, (padded, padded), 0) == lax.broadcasted_iota(
        jnp.int32, (padded, padded), 1
    )
    column = jnp.sum(
        jnp.where(same, jnp.broadcast_to(inverse[0:1], (padded, padded)), 0.0), 1, keepdims=True
    )
    squares[...] = jnp.broadcast_to(column, (padded, LANES))

    @pl.loop(0, rows // TILE)
    def _(tile):
        first = pl.multiple_of(tile * TILE, TILE)
        scale = squares[pl.ds(first, TILE), :]
        for group in range(groups):
            part = flat[pl.ds(first, TILE), lane_group(group)]
            out_ref[pl.ds(first, TILE), lane_group(group)] = (
                part * scale * gain_ref[:, lane_group(group)]
            ).astype(jnp.bfloat16)

    @pl.when(me < ctx_size - 1)
    def _():
        edge_copy.wait_send()
        for half in range(2):
            product_copy(half).wait_send()

    for step in range(1, ctx_size):
        @pl.when(me + step < ctx_size)
        def _():
            state_copy(step).wait_send()

    for step in range(1, ch_size):
        sum_copy(step).wait_send()


def on_device(
    ctx_size, ch_size, projected, short_filter, medium_filter, decay, residues, skip_gain, out_gain
):
    rows = projected.shape[1]
    chans = projected.shape[2]
    padded = -(-rows // LANES) * LANES
    f32 = jnp.float32
    bf16 = jnp.bfloat16

    def token_buffer(count, dtype=f32):
        return pltpu.VMEM((count * SUB, LANES), dtype)

    dma = pltpu.SemaphoreType.DMA
    vmem = pl.BlockSpec(memory_space=pltpu.VMEM)
    flops = rows * chans * (2 * MED + 6 * SHORT + 8 * MODES)
    return pl.pallas_call(
        functools.partial(block_kernel, ctx_size, ch_size),
        out_shape=pltpu.VMEM((rows, chans), bf16),
        in_specs=[pl.BlockSpec(memory_space=pltpu.HBM)] * 7,
        out_specs=vmem,
        scratch_shapes=[
            pltpu.VMEM(projected.shape, bf16),
            pltpu.VMEM((3, SHORT, chans), f32),
            pltpu.VMEM(medium_filter.shape, bf16),
            pltpu.VMEM(decay.shape, f32),
            pltpu.VMEM(residues.shape, f32),
            pltpu.VMEM((chans // LANES, LANES), f32),
            pltpu.VMEM((1, chans), f32),
            dma((9,)),
            token_buffer(LEAD + rows),
            token_buffer(LEAD + rows),
            token_buffer(LEAD + rows),
            token_buffer(SHORT * 3),
            pltpu.VMEM((SUBS, (DEPTH + rows // PHASES) * SUB, LANES), f32),
            pltpu.VMEM((SUBS, DEPTH * SUB, LANES), f32),
            pltpu.VMEM((SUBS, (1 + rows // PHASES) * SUB, LANES), f32),
            token_buffer(rows),
            token_buffer(rows),
            token_buffer(rows),
            token_buffer(MODES),
            token_buffer(MODES),
            token_buffer(MODES),
            token_buffer(MODES),
            token_buffer(TILE + 1),
            pltpu.VMEM((TILE, MODES * SUB, LANES), f32),
            pltpu.VMEM((rows // TILE, MODES * SUB, LANES), f32),
            pltpu.VMEM((rows, chans), f32),
            pltpu.VMEM((padded, LANES), f32),
            pltpu.VMEM((3, TILE, chans), bf16),
            pltpu.VMEM((2, MED * SUB // 2, LANES), bf16),
            pltpu.VMEM((2, MED * SUB // 2, LANES), bf16),
            token_buffer(MODES, bf16),
            pltpu.VMEM((ctx_size - 1, MODES * SUB, LANES), bf16),
            pltpu.VMEM((SUB, padded), f32),
            pltpu.VMEM((ch_size - 1, SUB, padded), f32),
            dma((2,)),
            dma((2, 2)),
            dma((ctx_size - 1,)),
            dma((ctx_size - 1,)),
            dma((ch_size - 1,)),
            dma((ch_size - 1,)),
        ],
        compiler_params=pltpu.CompilerParams(
            collective_id=0, has_side_effects=True, vmem_limit_bytes=40 * 1024 * 1024
        ),
        cost_estimate=pl.CostEstimate(
            flops=flops, bytes_accessed=rows * chans * 8, transcendentals=0
        ),
    )(
        *(
            pltpu.with_memory_space_constraint(operand, pltpu.HBM)
            for operand in (
                projected,
                jnp.transpose(short_filter, (1, 0, 2)),
                medium_filter,
                decay,
                residues,
                skip_gain.reshape(chans // LANES, LANES),
                out_gain.reshape(1, chans),
            )
        )
    )


def solution(mesh):
    in_specs = (
        P(None, "ctx", "ch"),
        P(None, None, "ch"),
        P(None, "ch"),
        P(None, "ch"),
        P(None, "ch"),
        P("ch"),
        P("ch"),
    )
    out_specs = P("ctx", "ch")
    body = functools.partial(on_device, mesh.shape["ctx"], mesh.shape["ch"])
    return jax.shard_map(
        body, mesh=mesh, in_specs=in_specs, out_specs=out_specs, check_vma=False
    )
```

```python
import functools

import jax
import jax.numpy as jnp
from jax import lax
from jax.experimental import pallas as pl
from jax.experimental.pallas import tpu as pltpu
from jax.sharding import PartitionSpec as P

C = 4096
SHORT = 7
MED = 128
MODES = 16
LANES = 128
SUB = 8
LEAD = 8
TILE = 16
TAPS = 8
PHASES = 4
SUBS = 9
DEPTH = MED // PHASES
norm_eps = 1e-06
MESH = pl.DeviceIdType.MESH


def as_tokens(rows):
    return rows.reshape(rows.shape[0] // SUB, SUB, LANES)


def as_rows(tokens):
    return tokens.reshape(tokens.shape[0] * SUB, LANES)


def token_rows(first, count):
    start = first * SUB
    if not isinstance(start, int):
        start = pl.multiple_of(start, SUB)
    return pl.ds(start, count * SUB)


def phase_parts(tokens):
    quads = tokens.reshape(tokens.shape[0] // PHASES, PHASES, SUB, LANES)
    part00, part10, part01, part11 = (quads[:, phase] for phase in range(PHASES))
    low, high = part00 + part10, part01 + part11
    parts = (
        part00, part01, part00 + part01,
        part10, part11, part10 + part11,
        low, high, low + high,
    )
    return [as_rows(part) for part in parts]


def gather_groups(parts):
    blank = jnp.zeros(parts[0].shape, jnp.float32)
    parts = list(parts) + [blank] * (SUB - len(parts))
    return jnp.transpose(jnp.stack(parts, 0), (1, 0, 2))


def rounded(tokens):
    return as_tokens(as_rows(tokens).astype(jnp.bfloat16).astype(jnp.float32))


def mode_sum(parts):
    count = parts.shape[0]
    while count > 1:
        count //= 2
        parts = parts[:count] + parts[count:]
    return parts[0]


def block_kernel(
    ctx_size,
    ch_size,
    proj_hbm,
    short_hbm,
    medium_hbm,
    decay_hbm,
    residue_hbm,
    skip_hbm,
    gain_hbm,
    out_ref,
    proj_ref,
    short_ref,
    medium_ref,
    decay_ref,
    residue_ref,
    skip_ref,
    gain_ref,
    load_sems,
    series0,
    series1,
    series2,
    short_taps,
    phased,
    phased_taps,
    filtered,
    queries,
    mediated,
    summed,
    rates,
    weights_buf,
    carry,
    block_decay,
    head_taps,
    out_table,
    entry_states,
    flat,
    squares,
    edge_recv,
    product_send,
    product_recv,
    state_send,
    state_recv,
    sum_send,
    sum_recv,
    edge_sems,
    product_sems,
    state_send_sems,
    state_recv_sems,
    sum_send_sems,
    sum_recv_sems,
):
    rows = proj_ref.shape[1]
    groups = proj_ref.shape[2] // LANES
    series = (series0, series1, series2)
    me = lax.axis_index("ctx")
    my_ch = lax.axis_index("ch")
    following = lax.rem(me + 1, ctx_size)

    pairs = {
        "short": (short_hbm, short_ref),
        "key": (proj_hbm.at[1], proj_ref.at[1]),
        "value": (proj_hbm.at[2], proj_ref.at[2]),
        "medium": (medium_hbm, medium_ref),
        "query": (proj_hbm.at[0], proj_ref.at[0]),
        "decay": (decay_hbm, decay_ref),
        "residue": (residue_hbm, residue_ref),
        "skip": (skip_hbm, skip_ref),
        "gain": (gain_hbm, gain_ref),
    }
    loads = {
        name: pltpu.make_async_copy(source, target, load_sems.at[position])
        for position, (name, (source, target)) in enumerate(pairs.items())
    }
    for load in loads.values():
        load.start()

    barrier = pltpu.get_barrier_semaphore()
    for step in range(1, ctx_size):
        pl.semaphore_signal(
            barrier,
            inc=1,
            device_id={"ctx": lax.rem(me + step, ctx_size)},
            device_id_type=MESH,
        )
    for step in range(1, ch_size):
        pl.semaphore_signal(
            barrier,
            inc=1,
            device_id={"ch": lax.rem(my_ch + step, ch_size)},
            device_id_type=MESH,
        )

    if groups < SUB:
        for ref in (
            series0, series1, series2, short_taps, rates, weights_buf,
        ):
            ref[...] = jnp.zeros(ref.shape, ref.dtype)

    def lane_group(group):
        return slice(group * LANES, (group + 1) * LANES)

    def spread_series(index, low, high):
        @pl.loop(low, high)
        def _(tile):
            first = pl.multiple_of(tile * TILE, TILE)
            tokens = gather_groups(
                [
                    proj_ref[index, pl.ds(first, TILE), lane_group(group)].astype(jnp.float32)
                    for group in range(groups)
                ]
            )
            series[index][token_rows(LEAD + first, TILE), :] = as_rows(tokens)

    loads["short"].wait()
    for index in range(3):
        for group in range(groups):
            short_taps[pl.ds(index * SHORT * SUB + group, SHORT, stride=SUB), :] = short_ref[
                index, :, lane_group(group)
            ]
    edge_copy = pltpu.make_async_remote_copy(
        src_ref=proj_hbm.at[:, pl.ds(rows - TILE, TILE), :],
        dst_ref=edge_recv,
        send_sem=edge_sems.at[0],
        recv_sem=edge_sems.at[1],
        device_id={"ctx": following},
        device_id_type=MESH,
    )
    half_tiles = MED // (2 * TILE)
    all_tiles = rows // TILE

    def product_copy(half):
        return pltpu.make_async_remote_copy(
            src_ref=product_send.at[half],
            dst_ref=product_recv.at[half],
            send_sem=product_sems.at[0, half],
            recv_sem=product_sems.at[1, half],
            device_id={"ctx": following},
            device_id_type=MESH,
        )

    def featured(index, first):
        window = as_tokens(series[index][token_rows(LEAD + first - (SHORT - 1), TILE + SHORT - 1), :])
        total = None
        for delay in range(SHORT):
            tap = short_taps[(index * SHORT + delay) * SUB : (index * SHORT + delay + 1) * SUB, :]
            offset = SHORT - 1 - delay
            term = tap[None] * window[offset : offset + TILE]
            total = term if total is None else total + term
        return rounded(total)

    def product_tile(first):
        return as_rows(featured(1, first) * featured(2, first)).astype(jnp.bfloat16)

    def keep_product(first, tokens):
        start = pl.multiple_of(first * (SUB // PHASES), TILE * SUB // PHASES)
        for sub, part in enumerate(phase_parts(tokens)):
            phased[sub, pl.ds(start, TILE * SUB // PHASES), :] = part

    def send_half(half):
        low = all_tiles - half_tiles * (half + 1)

        @pl.loop(low, low + half_tiles)
        def _(tile):
            first = tile * TILE
            value = product_tile(first)
            start = pl.multiple_of((tile - low) * (TILE * SUB), TILE * SUB)
            product_send[half, pl.ds(start, TILE * SUB), :] = value
            keep_product(MED + first, as_tokens(value.astype(jnp.float32)))

    def receive_half(half):
        @pl.when(me > 0)
        def _():
            product_copy(half).wait_recv()

            @pl.loop(0, half_tiles)
            def _(tile):
                start = pl.multiple_of(tile * TILE * SUB, TILE * SUB)
                part = product_recv[half, pl.ds(start, TILE * SUB), :].astype(jnp.float32)
                keep_product((tile + half_tiles * (1 - half)) * TILE, as_tokens(part))

    tail = all_tiles - half_tiles - 1
    loads["key"].wait()
    spread_series(1, tail, all_tiles)
    loads["value"].wait()
    spread_series(2, tail, all_tiles)
    send_half(0)
    pl.semaphore_wait(barrier, ctx_size - 1 + ch_size - 1)

    @pl.when(me < ctx_size - 1)
    def _():
        edge_copy.start()
        product_copy(0).start()

    middle = tail - half_tiles
    spread_series(1, middle, tail)
    spread_series(2, middle, tail)
    send_half(1)

    @pl.when(me < ctx_size - 1)
    def _():
        product_copy(1).start()

    spread_series(1, 0, middle)
    spread_series(2, 0, middle)
    loads["medium"].wait()

    @pl.loop(0, MED // TILE)
    def _(tile):
        first = pl.multiple_of(tile * TILE, TILE)
        taps = gather_groups(
            [
                medium_ref[pl.ds(first, TILE), lane_group(group)].astype(jnp.float32)
                for group in range(groups)
            ]
        )
        start = pl.multiple_of(tile * (TILE * SUB // PHASES), TILE * SUB // PHASES)
        for sub, part in enumerate(phase_parts(taps)):
            phased_taps[sub, pl.ds(start, TILE * SUB // PHASES), :] = part

    loads["decay"].wait()
    loads["residue"].wait()
    for group in range(groups):
        rate = decay_ref[:, lane_group(group)]
        twice = 2.0 * rate
        series_form = twice * (
            1.0
            - twice
            * (0.5 - twice * (1.0 / 6.0 - twice * (1.0 / 24.0 - twice * (1.0 / 120.0 - twice / 720.0))))
        )
        power = jnp.where(twice < 0.125, series_form, 1.0 - jnp.exp(-twice))
        rates[pl.ds(group, MODES, stride=SUB), :] = rate
        weights_buf[pl.ds(group, MODES, stride=SUB), :] = residue_ref[
            :, lane_group(group)
        ] * jnp.sqrt(power)

    @pl.when(me > 0)
    def _():
        edge_copy.wait_recv()
        for index in range(3):
            for group in range(groups):
                part = edge_recv[index, :, lane_group(group)].astype(jnp.float32)
                series[index][pl.ds(group, LEAD, stride=SUB), :] = part[TILE - LEAD :]

    @pl.when(me == 0)
    def _():
        for index in range(3):
            series[index][0 : LEAD * SUB, :] = jnp.zeros((LEAD * SUB, LANES), jnp.float32)

    @pl.loop(0, all_tiles - 2 * half_tiles)
    def _(tile):
        first = tile * TILE
        keep_product(MED + first, as_tokens(product_tile(first).astype(jnp.float32)))

    steps = rows // PHASES

    def sub_filter(sub, first, count):
        total = jnp.zeros((count, SUB, LANES), jnp.float32)
        for delay in range(0, DEPTH, TAPS):
            window = as_tokens(
                phased[sub, token_rows(DEPTH + first - delay - (TAPS - 1), count + TAPS - 1), :]
            )
            taps = as_tokens(phased_taps[sub, token_rows(delay, TAPS), :])
            for within in range(TAPS):
                offset = TAPS - 1 - within
                total = total + taps[within][None] * window[offset : offset + count]
        filtered[sub, token_rows(1 + first, count), :] = as_rows(total)

    def medium_tile(tile):
        @pl.loop(0, SUBS)
        def _(sub):
            sub_filter(sub, tile * TILE, TILE)

    def merge_tile(tile):
        count = TILE // PHASES
        first = tile * count
        wide = [
            as_tokens(filtered[sub, token_rows(first, count + 1), :]) for sub in range(SUBS)
        ]

        def half_rate(base):
            low, high, both = wide[base : base + 3]
            return low[1:] + high[:count], both - low - high

        even0, even1 = half_rate(0)
        odd0, odd1 = half_rate(3)
        both0, both1 = half_rate(6)
        outs = (
            even0 + odd1[:count],
            both0 - even0 - odd0,
            even1[1:] + odd0,
            (both1 - even1 - odd1)[1:],
        )
        tokens = jnp.stack(outs, 1).reshape(TILE, SUB, LANES)
        mediated[token_rows(tile * TILE, TILE), :] = as_rows(rounded(tokens))

    @pl.when(me == 0)
    def _():
        phased[:, 0 : DEPTH * SUB, :] = jnp.zeros((SUBS, DEPTH * SUB, LANES), jnp.float32)

    @pl.loop(DEPTH // TILE, steps // TILE)
    def _(tile):
        medium_tile(tile)

    for half in range(2):
        receive_half(half)
        medium_tile(1 - half)

    @pl.loop(0, SUBS)
    def _(sub):
        sub_filter(sub, -1, 1)

    @pl.loop(0, rows // TILE)
    def _(tile):
        merge_tile(tile)

    zero_state = jnp.zeros((MODES, SUB, LANES), jnp.float32)

    def state_step(block, state):
        entry_states[block] = as_rows(state)
        inputs = as_tokens(mediated[token_rows(block * TILE, TILE), :])
        step_decay = jnp.exp(-as_tokens(rates[...]))
        for within in range(TILE):
            state = step_decay * state + inputs[within][None]
        return state

    final = lax.fori_loop(0, all_tiles, state_step, zero_state)
    state_send[...] = as_rows(final).astype(jnp.bfloat16)

    def state_copy(step):
        return pltpu.make_async_remote_copy(
            src_ref=state_send,
            dst_ref=state_recv.at[step - 1],
            send_sem=state_send_sems.at[step - 1],
            recv_sem=state_recv_sems.at[step - 1],
            device_id={"ctx": lax.rem(me + step, ctx_size)},
            device_id_type=MESH,
        )

    for step in reversed(range(1, ctx_size)):
        @pl.when(me + step < ctx_size)
        def _():
            state_copy(step).start()

    loads["skip"].wait()
    loads["gain"].wait()
    skip = skip_ref[...]
    if groups < SUB:
        skip = jnp.concatenate([skip, jnp.zeros((SUB - groups, LANES), jnp.float32)], 0)

    decay_step = jnp.exp(-as_tokens(rates[...]))
    weights = as_tokens(weights_buf[...])
    block_decay[...] = jnp.exp(-float(TILE) * rates[...])
    head_taps[0:SUB, :] = mode_sum(weights) + skip

    def table_step(step, table):
        table = decay_step * table
        out_table[step] = as_rows(table)
        head_taps[token_rows(step + 1, 1), :] = mode_sum(table)
        return table

    lax.fori_loop(0, TILE, table_step, weights)

    loads["query"].wait()
    spread_series(0, 0, all_tiles)

    @pl.loop(0, rows // TILE)
    def _(tile):
        first = tile * TILE
        queries[token_rows(first, TILE), :] = as_rows(featured(0, first))

    @pl.loop(0, all_tiles)
    def _(block):
        inputs = as_tokens(mediated[token_rows(block * TILE, TILE), :])
        taps = as_tokens(head_taps[0 : TILE * SUB, :])
        sums = [taps[0] * inputs[step] for step in range(TILE)]
        for delay in range(1, TILE):
            for step in range(delay, TILE):
                sums[step] = sums[step] + taps[delay] * inputs[step - delay]
        summed[token_rows(block * TILE, TILE), :] = as_rows(jnp.stack(sums, 0))

    carry[...] = jnp.zeros(carry.shape, jnp.float32)
    for step in reversed(range(1, ctx_size)):
        @pl.when(me >= step)
        def _():
            state_copy(step).wait_recv()
            span = jnp.exp(-float(rows) * rates[...])
            carry[...] = carry[...] * span + state_recv[step - 1].astype(jnp.float32)

    @pl.loop(0, all_tiles // 2)
    def _(pair):
        states = []
        for member in range(2):
            arrived = carry[...]
            states.append(as_tokens(entry_states[pair * 2 + member] + arrived))
            carry[...] = arrived * block_decay[...]
        sums = ([], [])
        for step in range(TILE):
            table = as_tokens(out_table[step])
            for member in range(2):
                sums[member].append(mode_sum(table * states[member]))
        for member in range(2):
            here = token_rows((pair * 2 + member) * TILE, TILE)
            total = as_rows(jnp.stack(sums[member], 0)) + summed[here, :]
            summed[here, :] = queries[here, :] * total

    padded = squares.shape[0]
    if padded > rows:
        squares[rows:padded, :] = jnp.zeros((padded - rows, LANES), jnp.float32)

    @pl.loop(0, all_tiles)
    def _(tile):
        first = pl.multiple_of(tile * TILE, TILE)
        parts = jnp.transpose(as_tokens(summed[token_rows(first, TILE), :]), (1, 0, 2))
        total = None
        for group in range(groups):
            part = parts[group]
            total = part * part if total is None else total + part * part
            flat[pl.ds(first, TILE), lane_group(group)] = part
        squares[pl.ds(first, TILE), :] = total

    own_sum = lax.dot_general(
        jnp.ones((SUB, LANES), jnp.float32),
        squares[...],
        (((1,), (1,)), ((), ())),
        precision=lax.Precision.HIGHEST,
        preferred_element_type=jnp.float32,
    )
    sum_send[...] = own_sum

    def sum_copy(step):
        return pltpu.make_async_remote_copy(
            src_ref=sum_send,
            dst_ref=sum_recv.at[step - 1],
            send_sem=sum_send_sems.at[step - 1],
            recv_sem=sum_recv_sems.at[step - 1],
            device_id={"ch": lax.rem(my_ch + step, ch_size)},
            device_id_type=MESH,
        )

    for step in range(1, ch_size):
        sum_copy(step).start()
    total_sum = own_sum
    for step in range(1, ch_size):
        sum_copy(step).wait_recv()
        total_sum = total_sum + sum_recv[step - 1]
    inverse = lax.rsqrt(total_sum / C + norm_eps)
    same = lax.broadcasted_iota(jnp.int32, (padded, padded), 0) == lax.broadcasted_iota(
        jnp.int32, (padded, padded), 1
    )
    column = jnp.sum(
        jnp.where(same, jnp.broadcast_to(inverse[0:1], (padded, padded)), 0.0), 1, keepdims=True
    )
    squares[...] = jnp.broadcast_to(column, (padded, LANES))

    @pl.loop(0, rows // TILE)
    def _(tile):
        first = pl.multiple_of(tile * TILE, TILE)
        scale = squares[pl.ds(first, TILE), :]
        for group in range(groups):
            part = flat[pl.ds(first, TILE), lane_group(group)]
            out_ref[pl.ds(first, TILE), lane_group(group)] = (
                part * scale * gain_ref[:, lane_group(group)]
            ).astype(jnp.bfloat16)

    @pl.when(me < ctx_size - 1)
    def _():
        edge_copy.wait_send()
        for half in range(2):
            product_copy(half).wait_send()

    for step in range(1, ctx_size):
        @pl.when(me + step < ctx_size)
        def _():
            state_copy(step).wait_send()

    for step in range(1, ch_size):
        sum_copy(step).wait_send()


def on_device(
    ctx_size, ch_size, projected, short_filter, medium_filter, decay, residues, skip_gain, out_gain
):
    rows = projected.shape[1]
    chans = projected.shape[2]
    padded = -(-rows // LANES) * LANES
    f32 = jnp.float32
    bf16 = jnp.bfloat16

    def token_buffer(count, dtype=f32):
        return pltpu.VMEM((count * SUB, LANES), dtype)

    dma = pltpu.SemaphoreType.DMA
    vmem = pl.BlockSpec(memory_space=pltpu.VMEM)
    flops = rows * chans * (2 * MED + 6 * SHORT + 8 * MODES)
    return pl.pallas_call(
        functools.partial(block_kernel, ctx_size, ch_size),
        out_shape=pltpu.VMEM((rows, chans), bf16),
        in_specs=[pl.BlockSpec(memory_space=pltpu.HBM)] * 7,
        out_specs=vmem,
        scratch_shapes=[
            pltpu.VMEM(projected.shape, bf16),
            pltpu.VMEM((3, SHORT, chans), f32),
            pltpu.VMEM(medium_filter.shape, bf16),
            pltpu.VMEM(decay.shape, f32),
            pltpu.VMEM(residues.shape, f32),
            pltpu.VMEM((chans // LANES, LANES), f32),
            pltpu.VMEM((1, chans), f32),
            dma((9,)),
            token_buffer(LEAD + rows),
            token_buffer(LEAD + rows),
            token_buffer(LEAD + rows),
            token_buffer(SHORT * 3),
            pltpu.VMEM((SUBS, (DEPTH + rows // PHASES) * SUB, LANES), f32),
            pltpu.VMEM((SUBS, DEPTH * SUB, LANES), f32),
            pltpu.VMEM((SUBS, (1 + rows // PHASES) * SUB, LANES), f32),
            token_buffer(rows),
            token_buffer(rows),
            token_buffer(rows),
            token_buffer(MODES),
            token_buffer(MODES),
            token_buffer(MODES),
            token_buffer(MODES),
            token_buffer(TILE + 1),
            pltpu.VMEM((TILE, MODES * SUB, LANES), f32),
            pltpu.VMEM((rows // TILE, MODES * SUB, LANES), f32),
            pltpu.VMEM((rows, chans), f32),
            pltpu.VMEM((padded, LANES), f32),
            pltpu.VMEM((3, TILE, chans), bf16),
            pltpu.VMEM((2, MED * SUB // 2, LANES), bf16),
            pltpu.VMEM((2, MED * SUB // 2, LANES), bf16),
            token_buffer(MODES, bf16),
            pltpu.VMEM((ctx_size - 1, MODES * SUB, LANES), bf16),
            pltpu.VMEM((SUB, padded), f32),
            pltpu.VMEM((ch_size - 1, SUB, padded), f32),
            dma((2,)),
            dma((2, 2)),
            dma((ctx_size - 1,)),
            dma((ctx_size - 1,)),
            dma((ch_size - 1,)),
            dma((ch_size - 1,)),
        ],
        compiler_params=pltpu.CompilerParams(
            collective_id=0, has_side_effects=True, vmem_limit_bytes=40 * 1024 * 1024
        ),
        cost_estimate=pl.CostEstimate(
            flops=flops, bytes_accessed=rows * chans * 8, transcendentals=0
        ),
    )(
        *(
            pltpu.with_memory_space_constraint(operand, pltpu.HBM)
            for operand in (
                projected,
                jnp.transpose(short_filter, (1, 0, 2)),
                medium_filter,
                decay,
                residues,
                skip_gain.reshape(chans // LANES, LANES),
                out_gain.reshape(1, chans),
            )
        )
    )


def solution(mesh):
    in_specs = (
        P(None, "ctx", "ch"),
        P(None, None, "ch"),
        P(None, "ch"),
        P(None, "ch"),
        P(None, "ch"),
        P("ch"),
        P("ch"),
    )
    out_specs = P("ctx", "ch")
    body = functools.partial(on_device, mesh.shape["ctx"], mesh.shape["ch"])
    return jax.shard_map(
        body, mesh=mesh, in_specs=in_specs, out_specs=out_specs, check_vma=False
    )
```

```python
import functools

import jax
import jax.numpy as jnp
from jax import lax
from jax.experimental import pallas as pl
from jax.experimental.pallas import tpu as pltpu
from jax.sharding import PartitionSpec as P

C = 4096
SHORT = 7
MED = 128
MODES = 16
LANES = 128
SUB = 8
LEAD = 8
TILE = 16
TAPS = 8
PHASES = 4
SUBS = 9
DEPTH = MED // PHASES
norm_eps = 1e-06
MESH = pl.DeviceIdType.MESH


def as_tokens(rows):
    return rows.reshape(rows.shape[0] // SUB, SUB, LANES)


def as_rows(tokens):
    return tokens.reshape(tokens.shape[0] * SUB, LANES)


def token_rows(first, count):
    start = first * SUB
    if not isinstance(start, int):
        start = pl.multiple_of(start, SUB)
    return pl.ds(start, count * SUB)


def phase_parts(tokens):
    quads = tokens.reshape(tokens.shape[0] // PHASES, PHASES, SUB, LANES)
    part00, part10, part01, part11 = (quads[:, phase] for phase in range(PHASES))
    low, high = part00 + part10, part01 + part11
    parts = (
        part00, part01, part00 + part01,
        part10, part11, part10 + part11,
        low, high, low + high,
    )
    return [as_rows(part) for part in parts]


def gather_groups(parts):
    blank = jnp.zeros(parts[0].shape, jnp.float32)
    parts = list(parts) + [blank] * (SUB - len(parts))
    return jnp.transpose(jnp.stack(parts, 0), (1, 0, 2))


def rounded(tokens):
    return as_tokens(as_rows(tokens).astype(jnp.bfloat16).astype(jnp.float32))


def mode_sum(parts):
    count = parts.shape[0]
    while count > 1:
        count //= 2
        parts = parts[:count] + parts[count:]
    return parts[0]


def block_kernel(
    ctx_size,
    ch_size,
    proj_hbm,
    short_hbm,
    medium_hbm,
    decay_hbm,
    residue_hbm,
    skip_hbm,
    gain_hbm,
    out_ref,
    proj_ref,
    short_ref,
    medium_ref,
    decay_ref,
    residue_ref,
    skip_ref,
    gain_ref,
    load_sems,
    series0,
    series1,
    series2,
    short_taps,
    phased,
    phased_taps,
    filtered,
    queries,
    mediated,
    summed,
    rates,
    weights_buf,
    carry,
    block_decay,
    head_taps,
    out_table,
    entry_states,
    flat,
    squares,
    edge_recv,
    product_send,
    product_recv,
    state_send,
    state_recv,
    sum_send,
    sum_recv,
    edge_sems,
    product_sems,
    state_send_sems,
    state_recv_sems,
    sum_send_sems,
    sum_recv_sems,
):
    rows = proj_ref.shape[1]
    groups = proj_ref.shape[2] // LANES
    series = (series0, series1, series2)
    me = lax.axis_index("ctx")
    my_ch = lax.axis_index("ch")
    following = lax.rem(me + 1, ctx_size)

    pairs = {
        "short": (short_hbm, short_ref),
        "key": (proj_hbm.at[1], proj_ref.at[1]),
        "value": (proj_hbm.at[2], proj_ref.at[2]),
        "medium": (medium_hbm, medium_ref),
        "query": (proj_hbm.at[0], proj_ref.at[0]),
        "decay": (decay_hbm, decay_ref),
        "residue": (residue_hbm, residue_ref),
        "skip": (skip_hbm, skip_ref),
        "gain": (gain_hbm, gain_ref),
    }
    loads = {
        name: pltpu.make_async_copy(source, target, load_sems.at[position])
        for position, (name, (source, target)) in enumerate(pairs.items())
    }
    for load in loads.values():
        load.start()

    barrier = pltpu.get_barrier_semaphore()
    for step in range(1, ctx_size):
        pl.semaphore_signal(
            barrier,
            inc=1,
            device_id={"ctx": lax.rem(me + step, ctx_size)},
            device_id_type=MESH,
        )
    for step in range(1, ch_size):
        pl.semaphore_signal(
            barrier,
            inc=1,
            device_id={"ch": lax.rem(my_ch + step, ch_size)},
            device_id_type=MESH,
        )

    if groups < SUB:
        for ref in (
            series0, series1, series2, short_taps, rates, weights_buf,
        ):
            ref[...] = jnp.zeros(ref.shape, ref.dtype)

    def lane_group(group):
        return slice(group * LANES, (group + 1) * LANES)

    def spread_series(index, low, high):
        @pl.loop(low, high)
        def _(tile):
            first = pl.multiple_of(tile * TILE, TILE)
            tokens = gather_groups(
                [
                    proj_ref[index, pl.ds(first, TILE), lane_group(group)].astype(jnp.float32)
                    for group in range(groups)
                ]
            )
            series[index][token_rows(LEAD + first, TILE), :] = as_rows(tokens)

    loads["short"].wait()
    for index in range(3):
        for group in range(groups):
            short_taps[pl.ds(index * SHORT * SUB + group, SHORT, stride=SUB), :] = short_ref[
                index, :, lane_group(group)
            ]
    edge_copy = pltpu.make_async_remote_copy(
        src_ref=proj_hbm.at[:, pl.ds(rows - TILE, TILE), :],
        dst_ref=edge_recv,
        send_sem=edge_sems.at[0],
        recv_sem=edge_sems.at[1],
        device_id={"ctx": following},
        device_id_type=MESH,
    )
    half_tiles = MED // (2 * TILE)
    all_tiles = rows // TILE

    def product_copy(half):
        return pltpu.make_async_remote_copy(
            src_ref=product_send.at[half],
            dst_ref=product_recv.at[half],
            send_sem=product_sems.at[0, half],
            recv_sem=product_sems.at[1, half],
            device_id={"ctx": following},
            device_id_type=MESH,
        )

    def featured(index, first):
        window = as_tokens(series[index][token_rows(LEAD + first - (SHORT - 1), TILE + SHORT - 1), :])
        total = None
        for delay in range(SHORT):
            tap = short_taps[(index * SHORT + delay) * SUB : (index * SHORT + delay + 1) * SUB, :]
            offset = SHORT - 1 - delay
            term = tap[None] * window[offset : offset + TILE]
            total = term if total is None else total + term
        return rounded(total)

    def product_tile(first):
        return as_rows(featured(1, first) * featured(2, first)).astype(jnp.bfloat16)

    def keep_product(first, tokens):
        start = pl.multiple_of(first * (SUB // PHASES), TILE * SUB // PHASES)
        for sub, part in enumerate(phase_parts(tokens)):
            phased[sub, pl.ds(start, TILE * SUB // PHASES), :] = part

    def send_half(half):
        low = all_tiles - half_tiles * (half + 1)

        @pl.loop(low, low + half_tiles)
        def _(tile):
            first = tile * TILE
            value = product_tile(first)
            start = pl.multiple_of((tile - low) * (TILE * SUB), TILE * SUB)
            product_send[half, pl.ds(start, TILE * SUB), :] = value
            keep_product(MED + first, as_tokens(value.astype(jnp.float32)))

    def receive_half(half):
        @pl.when(me > 0)
        def _():
            product_copy(half).wait_recv()

            @pl.loop(0, half_tiles)
            def _(tile):
                start = pl.multiple_of(tile * TILE * SUB, TILE * SUB)
                part = product_recv[half, pl.ds(start, TILE * SUB), :].astype(jnp.float32)
                keep_product((tile + half_tiles * (1 - half)) * TILE, as_tokens(part))

    tail = all_tiles - half_tiles - 1
    loads["key"].wait()
    spread_series(1, tail, all_tiles)
    loads["value"].wait()
    spread_series(2, tail, all_tiles)
    send_half(0)
    pl.semaphore_wait(barrier, ctx_size - 1 + ch_size - 1)

    @pl.when(me < ctx_size - 1)
    def _():
        edge_copy.start()
        product_copy(0).start()

    middle = tail - half_tiles
    spread_series(1, middle, tail)
    spread_series(2, middle, tail)
    send_half(1)

    @pl.when(me < ctx_size - 1)
    def _():
        product_copy(1).start()

    spread_series(1, 0, middle)
    spread_series(2, 0, middle)
    loads["medium"].wait()

    @pl.loop(0, MED // TILE)
    def _(tile):
        first = pl.multiple_of(tile * TILE, TILE)
        taps = gather_groups(
            [
                medium_ref[pl.ds(first, TILE), lane_group(group)].astype(jnp.float32)
                for group in range(groups)
            ]
        )
        start = pl.multiple_of(tile * (TILE * SUB // PHASES), TILE * SUB // PHASES)
        for sub, part in enumerate(phase_parts(taps)):
            phased_taps[sub, pl.ds(start, TILE * SUB // PHASES), :] = part

    loads["decay"].wait()
    loads["residue"].wait()
    for group in range(groups):
        rate = decay_ref[:, lane_group(group)]
        twice = 2.0 * rate
        series_form = twice * (
            1.0
            - twice
            * (0.5 - twice * (1.0 / 6.0 - twice * (1.0 / 24.0 - twice * (1.0 / 120.0 - twice / 720.0))))
        )
        power = jnp.where(twice < 0.125, series_form, 1.0 - jnp.exp(-twice))
        rates[pl.ds(group, MODES, stride=SUB), :] = rate
        weights_buf[pl.ds(group, MODES, stride=SUB), :] = residue_ref[
            :, lane_group(group)
        ] * jnp.sqrt(power)

    @pl.when(me > 0)
    def _():
        edge_copy.wait_recv()
        for index in range(3):
            for group in range(groups):
                part = edge_recv[index, :, lane_group(group)].astype(jnp.float32)
                series[index][pl.ds(group, LEAD, stride=SUB), :] = part[TILE - LEAD :]

    @pl.when(me == 0)
    def _():
        for index in range(3):
            series[index][0 : LEAD * SUB, :] = jnp.zeros((LEAD * SUB, LANES), jnp.float32)

    @pl.loop(0, all_tiles - 2 * half_tiles)
    def _(tile):
        first = tile * TILE
        keep_product(MED + first, as_tokens(product_tile(first).astype(jnp.float32)))

    steps = rows // PHASES

    def sub_filter(sub, first, count):
        total = jnp.zeros((count, SUB, LANES), jnp.float32)
        for delay in range(0, DEPTH, TAPS):
            window = as_tokens(
                phased[sub, token_rows(DEPTH + first - delay - (TAPS - 1), count + TAPS - 1), :]
            )
            taps = as_tokens(phased_taps[sub, token_rows(delay, TAPS), :])
            for within in range(TAPS):
                offset = TAPS - 1 - within
                total = total + taps[within][None] * window[offset : offset + count]
        filtered[sub, token_rows(1 + first, count), :] = as_rows(total)

    def medium_tile(tile):
        @pl.loop(0, SUBS)
        def _(sub):
            sub_filter(sub, tile * TILE, TILE)

    def merge_tile(tile):
        count = TILE // PHASES
        first = tile * count
        wide = [
            as_tokens(filtered[sub, token_rows(first, count + 1), :]) for sub in range(SUBS)
        ]

        def half_rate(base):
            low, high, both = wide[base : base + 3]
            return low[1:] + high[:count], both - low - high

        even0, even1 = half_rate(0)
        odd0, odd1 = half_rate(3)
        both0, both1 = half_rate(6)
        outs = (
            even0 + odd1[:count],
            both0 - even0 - odd0,
            even1[1:] + odd0,
            (both1 - even1 - odd1)[1:],
        )
        tokens = jnp.stack(outs, 1).reshape(TILE, SUB, LANES)
        mediated[token_rows(tile * TILE, TILE), :] = as_rows(rounded(tokens))

    @pl.when(me == 0)
    def _():
        phased[:, 0 : DEPTH * SUB, :] = jnp.zeros((SUBS, DEPTH * SUB, LANES), jnp.float32)

    @pl.loop(DEPTH // TILE, steps // TILE)
    def _(tile):
        medium_tile(tile)

    for half in range(2):
        receive_half(half)
        medium_tile(1 - half)

    @pl.loop(0, SUBS)
    def _(sub):
        sub_filter(sub, -1, 1)

    @pl.loop(0, rows // TILE)
    def _(tile):
        merge_tile(tile)

    zero_state = jnp.zeros((MODES, SUB, LANES), jnp.float32)

    def state_step(block, state):
        entry_states[block] = as_rows(state)
        inputs = as_tokens(mediated[token_rows(block * TILE, TILE), :])
        step_decay = jnp.exp(-as_tokens(rates[...]))
        for within in range(TILE):
            state = step_decay * state + inputs[within][None]
        return state

    final = lax.fori_loop(0, all_tiles, state_step, zero_state)
    state_send[...] = as_rows(final).astype(jnp.bfloat16)

    def state_copy(step):
        return pltpu.make_async_remote_copy(
            src_ref=state_send,
            dst_ref=state_recv.at[step - 1],
            send_sem=state_send_sems.at[step - 1],
            recv_sem=state_recv_sems.at[step - 1],
            device_id={"ctx": lax.rem(me + step, ctx_size)},
            device_id_type=MESH,
        )

    for step in range(1, ctx_size):
        @pl.when(me + step < ctx_size)
        def _():
            state_copy(step).start()

    loads["skip"].wait()
    loads["gain"].wait()
    skip = skip_ref[...]
    if groups < SUB:
        skip = jnp.concatenate([skip, jnp.zeros((SUB - groups, LANES), jnp.float32)], 0)

    decay_step = jnp.exp(-as_tokens(rates[...]))
    weights = as_tokens(weights_buf[...])
    block_decay[...] = jnp.exp(-float(TILE) * rates[...])
    head_taps[0:SUB, :] = mode_sum(weights) + skip

    def table_step(step, table):
        table = decay_step * table
        out_table[step] = as_rows(table)
        head_taps[token_rows(step + 1, 1), :] = mode_sum(table)
        return table

    lax.fori_loop(0, TILE, table_step, weights)

    loads["query"].wait()
    spread_series(0, 0, all_tiles)

    @pl.loop(0, rows // TILE)
    def _(tile):
        first = tile * TILE
        queries[token_rows(first, TILE), :] = as_rows(featured(0, first))

    @pl.loop(0, all_tiles)
    def _(block):
        inputs = as_tokens(mediated[token_rows(block * TILE, TILE), :])
        taps = as_tokens(head_taps[0 : TILE * SUB, :])
        sums = [taps[0] * inputs[step] for step in range(TILE)]
        for delay in range(1, TILE):
            for step in range(delay, TILE):
                sums[step] = sums[step] + taps[delay] * inputs[step - delay]
        summed[token_rows(block * TILE, TILE), :] = as_rows(jnp.stack(sums, 0))

    carry[...] = jnp.zeros(carry.shape, jnp.float32)
    for step in reversed(range(1, ctx_size)):
        @pl.when(me >= step)
        def _():
            state_copy(step).wait_recv()
            span = jnp.exp(-float(rows) * rates[...])
            carry[...] = carry[...] * span + state_recv[step - 1].astype(jnp.float32)

    @pl.loop(0, all_tiles // 2)
    def _(pair):
        states = []
        for member in range(2):
            arrived = carry[...]
            states.append(as_tokens(entry_states[pair * 2 + member] + arrived))
            carry[...] = arrived * block_decay[...]
        sums = ([], [])
        for step in range(TILE):
            table = as_tokens(out_table[step])
            for member in range(2):
                sums[member].append(mode_sum(table * states[member]))
        for member in range(2):
            here = token_rows((pair * 2 + member) * TILE, TILE)
            total = as_rows(jnp.stack(sums[member], 0)) + summed[here, :]
            summed[here, :] = queries[here, :] * total

    padded = squares.shape[0]
    if padded > rows:
        squares[rows:padded, :] = jnp.zeros((padded - rows, LANES), jnp.float32)

    @pl.loop(0, all_tiles)
    def _(tile):
        first = pl.multiple_of(tile * TILE, TILE)
        parts = jnp.transpose(as_tokens(summed[token_rows(first, TILE), :]), (1, 0, 2))
        total = None
        for group in range(groups):
            part = parts[group]
            total = part * part if total is None else total + part * part
            flat[pl.ds(first, TILE), lane_group(group)] = part
        squares[pl.ds(first, TILE), :] = total

    own_sum = lax.dot_general(
        jnp.ones((SUB, LANES), jnp.float32),
        squares[...],
        (((1,), (1,)), ((), ())),
        precision=lax.Precision.HIGHEST,
        preferred_element_type=jnp.float32,
    )
    sum_send[...] = own_sum

    def sum_copy(step):
        return pltpu.make_async_remote_copy(
            src_ref=sum_send,
            dst_ref=sum_recv.at[step - 1],
            send_sem=sum_send_sems.at[step - 1],
            recv_sem=sum_recv_sems.at[step - 1],
            device_id={"ch": lax.rem(my_ch + step, ch_size)},
            device_id_type=MESH,
        )

    for step in range(1, ch_size):
        sum_copy(step).start()
    total_sum = own_sum
    for step in range(1, ch_size):
        sum_copy(step).wait_recv()
        total_sum = total_sum + sum_recv[step - 1]
    inverse = lax.rsqrt(total_sum / C + norm_eps)
    same = lax.broadcasted_iota(jnp.int32, (padded, padded), 0) == lax.broadcasted_iota(
        jnp.int32, (padded, padded), 1
    )
    column = jnp.sum(
        jnp.where(same, jnp.broadcast_to(inverse[0:1], (padded, padded)), 0.0), 1, keepdims=True
    )
    squares[...] = jnp.broadcast_to(column, (padded, LANES))

    @pl.loop(0, rows // TILE)
    def _(tile):
        first = pl.multiple_of(tile * TILE, TILE)
        scale = squares[pl.ds(first, TILE), :]
        for group in range(groups):
            part = flat[pl.ds(first, TILE), lane_group(group)]
            out_ref[pl.ds(first, TILE), lane_group(group)] = (
                part * scale * gain_ref[:, lane_group(group)]
            ).astype(jnp.bfloat16)

    @pl.when(me < ctx_size - 1)
    def _():
        edge_copy.wait_send()
        for half in range(2):
            product_copy(half).wait_send()

    for step in range(1, ctx_size):
        @pl.when(me + step < ctx_size)
        def _():
            state_copy(step).wait_send()

    for step in range(1, ch_size):
        sum_copy(step).wait_send()


def on_device(
    ctx_size, ch_size, projected, short_filter, medium_filter, decay, residues, skip_gain, out_gain
):
    rows = projected.shape[1]
    chans = projected.shape[2]
    padded = -(-rows // LANES) * LANES
    f32 = jnp.float32
    bf16 = jnp.bfloat16

    def token_buffer(count, dtype=f32):
        return pltpu.VMEM((count * SUB, LANES), dtype)

    dma = pltpu.SemaphoreType.DMA
    vmem = pl.BlockSpec(memory_space=pltpu.VMEM)
    flops = rows * chans * (2 * MED + 6 * SHORT + 8 * MODES)
    return pl.pallas_call(
        functools.partial(block_kernel, ctx_size, ch_size),
        out_shape=pltpu.VMEM((rows, chans), bf16),
        in_specs=[pl.BlockSpec(memory_space=pltpu.HBM)] * 7,
        out_specs=vmem,
        scratch_shapes=[
            pltpu.VMEM(projected.shape, bf16),
            pltpu.VMEM((3, SHORT, chans), f32),
            pltpu.VMEM(medium_filter.shape, bf16),
            pltpu.VMEM(decay.shape, f32),
            pltpu.VMEM(residues.shape, f32),
            pltpu.VMEM((chans // LANES, LANES), f32),
            pltpu.VMEM((1, chans), f32),
            dma((9,)),
            token_buffer(LEAD + rows),
            token_buffer(LEAD + rows),
            token_buffer(LEAD + rows),
            token_buffer(SHORT * 3),
            pltpu.VMEM((SUBS, (DEPTH + rows // PHASES) * SUB, LANES), f32),
            pltpu.VMEM((SUBS, DEPTH * SUB, LANES), f32),
            pltpu.VMEM((SUBS, (1 + rows // PHASES) * SUB, LANES), f32),
            token_buffer(rows),
            token_buffer(rows),
            token_buffer(rows),
            token_buffer(MODES),
            token_buffer(MODES),
            token_buffer(MODES),
            token_buffer(MODES),
            token_buffer(TILE + 1),
            pltpu.VMEM((TILE, MODES * SUB, LANES), f32),
            pltpu.VMEM((rows // TILE, MODES * SUB, LANES), f32),
            pltpu.VMEM((rows, chans), f32),
            pltpu.VMEM((padded, LANES), f32),
            pltpu.VMEM((3, TILE, chans), bf16),
            pltpu.VMEM((2, MED * SUB // 2, LANES), bf16),
            pltpu.VMEM((2, MED * SUB // 2, LANES), bf16),
            token_buffer(MODES, bf16),
            pltpu.VMEM((ctx_size - 1, MODES * SUB, LANES), bf16),
            pltpu.VMEM((SUB, padded), f32),
            pltpu.VMEM((ch_size - 1, SUB, padded), f32),
            dma((2,)),
            dma((2, 2)),
            dma((ctx_size - 1,)),
            dma((ctx_size - 1,)),
            dma((ch_size - 1,)),
            dma((ch_size - 1,)),
        ],
        compiler_params=pltpu.CompilerParams(
            collective_id=0, has_side_effects=True, vmem_limit_bytes=40 * 1024 * 1024
        ),
        cost_estimate=pl.CostEstimate(
            flops=flops, bytes_accessed=rows * chans * 8, transcendentals=0
        ),
    )(
        *(
            pltpu.with_memory_space_constraint(operand, pltpu.HBM)
            for operand in (
                projected,
                jnp.transpose(short_filter, (1, 0, 2)),
                medium_filter,
                decay,
                residues,
                skip_gain.reshape(chans // LANES, LANES),
                out_gain.reshape(1, chans),
            )
        )
    )


def solution(mesh):
    in_specs = (
        P(None, "ctx", "ch"),
        P(None, None, "ch"),
        P(None, "ch"),
        P(None, "ch"),
        P(None, "ch"),
        P("ch"),
        P("ch"),
    )
    out_specs = P("ctx", "ch")
    body = functools.partial(on_device, mesh.shape["ctx"], mesh.shape["ch"])
    return jax.shard_map(
        body, mesh=mesh, in_specs=in_specs, out_specs=out_specs, check_vma=False
    )
```
